512 devices in a mesh: dp: 64 (over y, x, core), tensor: 8 (over z).
Axes of the slice: x: 4, y: 8, z: 8, core: 2. Of those that a mesh axis runs over, the one named last changes fastest.
Arguments:
- queries: bfloat16 [2, 8192, 2048], P(None, 'dp', 'tensor'), may hold values from -5 to 5
- key_rows: bfloat16 [2, 8192, 2048], P(None, 'dp', 'tensor'), may hold values from -5 to 5
- value_rows: bfloat16 [2, 8192, 2048], P(None, 'dp', 'tensor'), may hold values from -5 to 5
- out_weight: bfloat16 [2048, 2048], P('tensor'), may hold values from -0.125 to 0.125
- out_grad: bfloat16 [2, 8192, 2048], P(None, 'dp', 'tensor'), may hold values from -16 to 16
- ibd_lists: int32 [2, 64, 9], replicated, may hold values from 0 to 63, as said below
- ibd_counts: int32 [2, 64], replicated, may hold values from 1 to 9, as said below
Outputs:
- layer_out: bfloat16 [2, 8192, 2048], P(None, 'dp', 'tensor')
- query_grad: bfloat16 [2, 8192, 2048], P(None, 'dp', 'tensor')
- key_grad: bfloat16 [2, 8192, 2048], P(None, 'dp', 'tensor')
- value_grad: bfloat16 [2, 8192, 2048], P(None, 'dp', 'tensor')
- proj_grad: float32 [2048, 2048], P('dp', 'tensor')
The draws below stay inside these ranges and needn't reach their ends.
Inputs may be any that keep to these rules, and one draw needn't show every extreme that they name: The first ibd_counts[v, i] entries of ibd_lists[v, i] are distinct blocks within 4 blocks of i, the first being i itself; later entries repeat i. A block other than i is among the live entries of ibd_lists[v, i] for at most one variant v. ibd_counts[v, i] is at most the number of blocks within 4 blocks of i, i included.
All inputs are finite; a program needn't handle non-finite values.
Results may differ from the reference program's by a relative error of at most 0.017.
Values may be sent and summed in bfloat16 or wider, within the bound.
A program may use at most 64 MiB of HBM per device.

```python
import math
import jax
import jax.numpy as jnp
from jax import lax

D = 2048
NH = 16
HD = 128
VARS = 2
BLOCK = 128
REACH = 4
BLOCKS = 64
HAPS = 8192
N_TENSOR = 8


def ibd_plan(key):
    key = jax.random.fold_in(key, 101)
    order_key, length_key, full_key, owner_key = jax.random.split(key, 4)
    window_span = 2 * REACH + 1
    block_ids = jnp.arange(BLOCKS, dtype=jnp.int32)
    spot_index = jnp.arange(window_span, dtype=jnp.int32)
    variant_ids = jnp.arange(VARS, dtype=jnp.int32)
    candidates = block_ids[:, None] + spot_index[None, :] - REACH
    inside = (candidates >= 0) & (candidates < BLOCKS)
    is_self = candidates == block_ids[:, None]
    longest = jax.random.randint(full_key, (), REACH, BLOCKS - REACH)
    owner = jax.random.randint(owner_key, (BLOCKS, window_span), 0, VARS)
    owner = jnp.where(block_ids[:, None] == longest, 0, owner)
    owned = (owner[None, :, :] == variant_ids[:, None, None]) & inside[None] & jnp.logical_not(is_self)[None]
    jitter_values = jax.random.randint(order_key, (VARS, BLOCKS, window_span), 0, 1 << 20) * 16 + spot_index
    priority = jnp.where(owned, jitter_values, (1 << 25) + spot_index)
    priority = jnp.where(inside[None], priority, (1 << 26) + spot_index)
    priority = jnp.where(is_self[None], -1, priority)
    ranking = jnp.argsort(priority, axis=-1, stable=True)
    chosen = jnp.take_along_axis(jnp.broadcast_to(candidates, (VARS, BLOCKS, window_span)), ranking, axis=-1)
    usable = 1 + jnp.sum(owned.astype(jnp.int32), axis=-1)
    length_draws = jax.random.randint(length_key, (VARS, BLOCKS), 0, 256)
    lengths = 1 + length_draws * length_draws * usable // 65536
    full_spot = (variant_ids[:, None] == 0) & (block_ids[None, :] == longest)
    lengths = jnp.where(full_spot, usable, lengths)
    ibd_lists = jnp.where(spot_index[None, None, :] < lengths[:, :, None], chosen, block_ids[None, :, None])
    return (ibd_lists.astype(jnp.int32), lengths.astype(jnp.int32))


def draw_ibd_lists(key, part):
    return ibd_plan(key)[0]


def draw_ibd_counts(key, part):
    return ibd_plan(key)[1]


def draw_key_rows(key, part):
    key = jax.random.fold_in(key, 5)
    field = jax.random.normal(key, (VARS, HAPS, NH * HD), jnp.float32)
    return jnp.clip(field, -5.0, 5.0).astype(jnp.bfloat16)


def draw_queries(key, part):
    key = jax.random.fold_in(key, 29)
    field = jax.random.normal(key, (VARS, HAPS, NH * HD), jnp.float32)
    return jnp.clip(field, -5.0, 5.0).astype(jnp.bfloat16)


def spiked(array, own_key, source, target, shards_of, factor):
    owner, partner = [(jnp.arange(array.shape[position]) // (array.shape[position] // shards_of)).reshape([-1 if axis == position else 1 for axis in range(array.ndim)]) for position in (source, target)]
    chosen = jax.random.permutation(own_key, shards_of)[partner]
    strong = (owner == chosen) | (owner == (partner + shards_of // 2) % shards_of)
    return jnp.where(strong, factor * array, array)


def block_levels(rng, extent, shards, least, largest):
    factor_of, own = 1.0, jax.random.fold_in(rng, 6)
    for dim, shards_of in shards:
        heights = jnp.exp(jax.random.uniform(jax.random.fold_in(own, dim), (shards_of,), jnp.float32, least / len(shards), largest / len(shards)))
        factor_of = factor_of * jnp.repeat(heights, extent[dim] // shards_of).reshape([-1 if axis == dim else 1 for axis in range(len(extent))])
    return factor_of


def normal_values(own_key, extent, deviation, limit, cuts=(), held_as=jnp.bfloat16):
    loudness = block_levels(own_key, extent, cuts, -0.22, 0.18) if cuts else 1.0
    values = jax.random.normal(own_key, extent, jnp.float32) * deviation * loudness
    return jnp.minimum(jnp.maximum(values, -limit), limit).astype(held_as)


def noise_with(key, extent, width, limit, cuts, heavy, held_as=jnp.bfloat16):
    entries = width * jax.random.normal(key, extent, jnp.float32)
    if cuts:
        entries = entries * block_levels(key, extent, cuts, -0.22, 0.18)
    return jnp.clip(spiked(entries, jax.random.fold_in(key, 3), *heavy), -limit, limit).astype(held_as)


def setup_inputs(seed: int = 0) -> dict:
    key_list = jax.random.split(jax.random.key(seed), 8)
    return {
        "queries": draw_queries(jax.random.fold_in(key_list[7], 71), 0),
        "key_rows": draw_key_rows(jax.random.fold_in(key_list[7], 71), 0),
        "value_rows": normal_values(key_list[2], (VARS, HAPS, NH * HD), 1.0, 5.0, ((1, 64), (2, 8))),
        "out_weight": normal_values(key_list[3], (NH * HD, D), (NH * HD) ** -0.5, 0.125, ((0, 8),)),
        "out_grad": noise_with(key_list[4], (VARS, HAPS, D), 1.0, 16.0, ((1, 64), (2, 8)), (1, 2, 64, 4.0)),
        "ibd_lists": draw_ibd_lists(jax.random.fold_in(key_list[7], 71), 0),
        "ibd_counts": draw_ibd_counts(jax.random.fold_in(key_list[7], 71), 0),
    }


NEGATIVE = -1e+30

def as_heads(source):
    return source.reshape(source.shape[0], source.shape[1], NH, HD).astype(jnp.float32)

def rounded(source):
    return lax.optimization_barrier(source.astype(jnp.bfloat16)).astype(jnp.float32)

def listed_blocks(ibd_lists, ibd_counts):
    window_span = 2 * REACH + 1
    slot_index = jnp.arange(ibd_lists.shape[2], dtype=jnp.int32)
    live_slots = slot_index[None, None, :] < ibd_counts[:, :, None]
    targets = jnp.arange(BLOCKS, dtype=jnp.int32)[:, None] + jnp.arange(window_span, dtype=jnp.int32)[None, :] - REACH
    matches = (ibd_lists[:, :, :, None] == targets[None, :, None, :]) & live_slots[:, :, :, None]
    return jnp.any(matches, axis=2)

def weights_from(scores, keep_mask):
    highest = lax.optimization_barrier(jnp.max(jnp.where(keep_mask, scores, NEGATIVE), axis=-1, keepdims=True))
    totals = lax.optimization_barrier(jnp.sum(jnp.where(keep_mask, jnp.exp(scores - highest), 0.0), axis=-1, keepdims=True))
    log_totals = highest + jnp.log(totals)
    return (jnp.where(keep_mask, jnp.exp(scores - log_totals), 0.0), log_totals[..., 0])

def reference(queries, key_rows, value_rows, out_weight, out_grad, ibd_lists, ibd_counts):
    window_span = 2 * REACH + 1
    features = NH * HD
    score_scale = 1.0 / math.sqrt(HD)
    rim_rows = REACH * BLOCK
    listed = listed_blocks(ibd_lists, ibd_counts)
    padded_listed = jnp.pad(listed, ((0, 0), (REACH, REACH), (0, 0)))
    listing = jnp.stack([padded_listed[:, offset:offset + BLOCKS, window_span - 1 - offset] for offset in range(window_span)], axis=-1)

    def widen_rows(source):
        return jnp.pad(source, ((0, 0), (rim_rows, rim_rows), (0, 0)))

    def widen_last(source):
        return jnp.pad(source, ((0, 0), (0, 0), (rim_rows, rim_rows)))
    key_pad = widen_rows(key_rows)
    value_pad = widen_rows(value_rows)

    def window_of(source, block_index):
        return as_heads(lax.dynamic_slice_in_dim(source, block_index * BLOCK, window_span * BLOCK, 1))

    def block_of(source, block_index):
        return as_heads(lax.dynamic_slice_in_dim(source, block_index * BLOCK, BLOCK, 1))

    def key_mask(block_index):
        list_rows = lax.dynamic_index_in_dim(listed, block_index, 1, keepdims=False)
        return jnp.repeat(list_rows, BLOCK, axis=1)[:, None, None, :]

    def forward(block_index):
        scores = jnp.einsum('vqhd,vkhd->vhqk', block_of(queries, block_index), window_of(key_pad, block_index)) * score_scale
        prob_rows, log_totals = weights_from(scores, key_mask(block_index))
        attended = jnp.einsum('vhqk,vkhd->vqhd', rounded(prob_rows), window_of(value_pad, block_index))
        return (attended.astype(jnp.bfloat16), log_totals)
    block_ids = jnp.arange(BLOCKS, dtype=jnp.int32)
    attended_blocks, log_blocks = lax.map(forward, block_ids)
    attended = jnp.transpose(attended_blocks, (1, 0, 2, 3, 4)).reshape(VARS, HAPS, features)
    attended = lax.optimization_barrier(attended)
    log_totals = jnp.transpose(log_blocks, (1, 2, 0, 3)).reshape(VARS, NH, HAPS)
    flat_attended = attended.reshape(VARS * HAPS, features)
    group_width = features // N_TENSOR
    summed = jnp.zeros((VARS * HAPS, D), jnp.float32)
    for group_index in range(N_TENSOR):
        columns = slice(group_index * group_width, (group_index + 1) * group_width)
        group_term = jnp.dot(flat_attended[:, columns], out_weight[columns], preferred_element_type=jnp.float32)
        summed = summed + rounded(group_term)
    layer_out = summed.astype(jnp.bfloat16).reshape(VARS, HAPS, D)
    flat_grad = out_grad.reshape(VARS * HAPS, D)
    attended_grad = jnp.dot(flat_grad, out_weight.T, preferred_element_type=jnp.float32).astype(jnp.bfloat16)
    attended_grad = lax.optimization_barrier(attended_grad.reshape(VARS, HAPS, features))
    proj_grad = jnp.dot(flat_grad.T, flat_attended, preferred_element_type=jnp.float32)

    def query_side(block_index):
        key_heads = window_of(key_pad, block_index)
        scores = jnp.einsum('vqhd,vkhd->vhqk', block_of(queries, block_index), key_heads) * score_scale
        log_rows = lax.dynamic_index_in_dim(log_blocks, block_index, 0, keepdims=False)
        prob_rows = jnp.where(key_mask(block_index), jnp.exp(scores - log_rows[..., None]), 0.0)
        prob_grads = jnp.einsum('vqhd,vkhd->vhqk', block_of(attended_grad, block_index), window_of(value_pad, block_index))
        deltas = lax.optimization_barrier(jnp.sum(prob_rows * prob_grads, axis=-1))
        score_grads = rounded(prob_rows * (prob_grads - deltas[..., None]) * score_scale)
        query_part = jnp.einsum('vhqk,vkhd->vqhd', score_grads, key_heads)
        return (query_part.astype(jnp.bfloat16), deltas)
    query_blocks, delta_blocks = lax.map(query_side, block_ids)
    query_grad = jnp.transpose(query_blocks, (1, 0, 2, 3, 4)).reshape(VARS, HAPS, features)
    deltas = jnp.transpose(delta_blocks, (1, 2, 0, 3)).reshape(VARS, NH, HAPS)
    query_pad = widen_rows(queries)
    grad_pad = widen_rows(attended_grad)
    log_pad = widen_last(log_totals)
    delta_pad = widen_last(deltas)

    def key_side(block_index):
        near_queries = window_of(query_pad, block_index)
        near_grads = window_of(grad_pad, block_index)
        near_logs = lax.dynamic_slice_in_dim(log_pad, block_index * BLOCK, window_span * BLOCK, 2)
        near_deltas = lax.dynamic_slice_in_dim(delta_pad, block_index * BLOCK, window_span * BLOCK, 2)
        list_rows = lax.dynamic_index_in_dim(listing, block_index, 1, keepdims=False)
        keep_mask = jnp.repeat(list_rows, BLOCK, axis=1)[:, None, :, None]
        scores = jnp.einsum('vqhd,vkhd->vhqk', near_queries, block_of(key_rows, block_index)) * score_scale
        prob_rows = jnp.where(keep_mask, jnp.exp(scores - near_logs[..., None]), 0.0)
        value_part = jnp.einsum('vhqk,vqhd->vkhd', rounded(prob_rows), near_grads)
        prob_grads = jnp.einsum('vqhd,vkhd->vhqk', near_grads, block_of(value_rows, block_index))
        score_grads = rounded(prob_rows * (prob_grads - near_deltas[..., None]) * score_scale)
        key_part = jnp.einsum('vhqk,vqhd->vkhd', score_grads, near_queries)
        return (key_part.astype(jnp.bfloat16), value_part.astype(jnp.bfloat16))
    key_blocks, value_blocks = lax.map(key_side, block_ids)
    key_grad = jnp.transpose(key_blocks, (1, 0, 2, 3, 4)).reshape(VARS, HAPS, features)
    value_grad = jnp.transpose(value_blocks, (1, 0, 2, 3, 4)).reshape(VARS, HAPS, features)
    return (layer_out, query_grad, key_grad, value_grad, proj_grad)
```

```python
import functools
import math

import jax
import jax.numpy as jnp
from jax import lax
from jax.experimental import pallas as pl
from jax.experimental.pallas import tpu as pltpu
from jax.sharding import PartitionSpec as P

HD = 128
REACH = 4
NEGATIVE = -1e30
RING = 8
ROW = 4
MESH = pl.DeviceIdType.MESH
VMEM = pltpu.VMEM
F32 = jnp.float32
BF16 = jnp.bfloat16

OFFSETS = tuple(o for o in range(-REACH, REACH + 1) if o != 0)
FAR_FIRST = tuple(sorted(OFFSETS, key=lambda o: -abs(o)))


def slot_of(offset):
    return offset + REACH if offset < 0 else offset + REACH - 1


def wrap(index, size):
    return lax.rem(index + size, size)


def dot_nn(a, b):
    return lax.dot_general(a, b, (((1,), (0,)), ((), ())), preferred_element_type=F32)


def dot_nt(a, b):
    return lax.dot_general(a, b, (((1,), (1,)), ((), ())), preferred_element_type=F32)


def dot_tn(a, b):
    return lax.dot_general(a, b, (((0,), (0,)), ((), ())), preferred_element_type=F32)


def lists_block(lists_ref, counts_ref, variant, row, block):
    count = counts_ref[variant, row]
    hit = jnp.int32(0)
    for slot in range(lists_ref.shape[2]):
        same = (lists_ref[variant, row, slot] == block) & (count > slot)
        hit = jnp.where(same, 1, hit)
    return hit


def greet(partners):
    barrier = pltpu.get_barrier_semaphore()
    for partner in partners:
        pl.semaphore_signal(barrier, inc=1, device_id=partner, device_id_type=MESH)
    pl.semaphore_wait(barrier, len(partners))


def fetch_kernel(
    lists_ref, counts_ref, k_ref, v_ref, og_ref, win_ref, full_ref,
    picked, kv_send, kv_recv, ring_send, ring_recv, own_sem,
):
    d = lax.axis_index("dp")
    t = lax.axis_index("tensor")
    n_dp = lax.axis_size("dp")
    sides = ((0, -1), (1, 1))
    near = [(wrap(d + o, n_dp), t) for o in OFFSETS]
    beside = [(d, wrap(t + step, RING)) for _, step in sides]
    own = pltpu.make_async_copy(og_ref, full_ref.at[t], own_sem)
    own.start()
    greet(near + beside)

    def hop(side, step, distance, half):
        source = wrap(t - step * (distance - 1), RING)
        origin = og_ref.at[half] if distance == 1 else full_ref.at[source, half]
        return pltpu.make_async_remote_copy(
            src_ref=origin,
            dst_ref=full_ref.at[source, half],
            send_sem=ring_send.at[side, distance - 1, half],
            recv_sem=ring_recv.at[side, distance - 1, half],
            device_id=(d, wrap(t + step, RING)),
            device_id_type=MESH,
        )

    hops = {}
    for half in range(2):
        for side, step in sides:
            hops[side, 1, half] = hop(side, step, 1, half)
            hops[side, 1, half].start()

    sends = []
    for o in FAR_FIRST:
        e = wrap(d + o, n_dp)
        slot = slot_of(o)
        second = lists_block(lists_ref, counts_ref, 1, e, d) == 1
        picked[slot, 0] = jnp.where(second, k_ref[1], k_ref[0])
        picked[slot, 1] = jnp.where(second, v_ref[1], v_ref[0])
        copy = pltpu.make_async_remote_copy(
            src_ref=picked.at[slot],
            dst_ref=win_ref.at[slot_of(-o)],
            send_sem=kv_send.at[slot],
            recv_sem=kv_recv.at[slot_of(-o)],
            device_id=(e, t),
            device_id_type=MESH,
        )
        copy.start()
        sends.append(copy)

    for distance in range(1, 4):
        for half in range(2):
            for side, step in sides:
                hops[side, distance, half].wait_recv()
                if distance < 3 or half == side:
                    hops[side, distance + 1, half] = hop(side, step, distance + 1, half)
                    hops[side, distance + 1, half].start()
    for side in range(2):
        hops[side, 4, side].wait_recv()
    for copy in hops.values():
        copy.wait_send()
    for copy in sends:
        copy.wait()
    own.wait()


def attend_kernel(
    lists_ref, counts_ref, q_ref, k_ref, v_ref, w_ref, win_ref, full_ref,
    dq_ref, own_ref, term_ref, part_ref, proj_ref,
    grad, scores, prob_grads, attended,
):
    d = lax.axis_index("dp")
    scale = 1.0 / math.sqrt(HD)
    width = q_ref.shape[2]
    heads = width // HD
    variants = q_ref.shape[0]
    rows = q_ref.shape[1]

    total = jnp.zeros((variants * rows, width), F32)
    for z in range(RING):
        block = full_ref[z].reshape(variants * rows, width)
        total = total + dot_nt(block, w_ref[:, z * width:(z + 1) * width])
    grad[...] = total.astype(BF16).reshape(variants, rows, width)

    pairs = [(None, v) for v in range(variants)]
    for o in OFFSETS:
        first = lists_block(lists_ref, counts_ref, 0, d, d + o)
        second = lists_block(lists_ref, counts_ref, 1, d, d + o)
        pairs.append((o, (second, (first + second) > 0)))

    def cols(h):
        return slice(h * HD, (h + 1) * HD)

    def key_of(pair, h):
        o, which = pair
        return k_ref[which, :, cols(h)] if o is None else win_ref[slot_of(o), 0, :, cols(h)]

    def value_of(pair, h):
        o, which = pair
        return v_ref[which, :, cols(h)] if o is None else win_ref[slot_of(o), 1, :, cols(h)]

    def of_variant(pair, ref, h):
        o, which = pair
        return ref[which if o is None else which[0], :, cols(h)]

    def pick(pair, stats):
        o, which = pair
        return stats[which] if o is None else jnp.where(which[0] == 1, stats[1], stats[0])

    def merge(pair, stats, new, combine, neutral):
        o, which = pair
        if o is None:
            stats[which] = combine(stats[which], new)
        else:
            for v in range(variants):
                stats[v] = combine(stats[v], jnp.where(which[0] == v, new, neutral))

    for h in range(heads):
        tops = [jnp.full((1, rows), NEGATIVE, F32) for _ in range(variants)]
        for p, pair in enumerate(pairs):
            s = dot_nt(key_of(pair, h), of_variant(pair, q_ref, h)) * scale
            if pair[0] is not None:
                s = jnp.where(pair[1][1], s, NEGATIVE)
            scores[p, h] = s
            merge(pair, tops, jnp.max(s, axis=0, keepdims=True), jnp.maximum, NEGATIVE)
            prob_grads[p, h] = dot_nt(value_of(pair, h), of_variant(pair, grad, h))
        sums = [jnp.zeros((1, rows), F32) for _ in range(variants)]
        for p, pair in enumerate(pairs):
            e = jnp.exp(scores[p, h] - pick(pair, tops))
            scores[p, h] = e
            merge(pair, sums, jnp.sum(e, axis=0, keepdims=True), jnp.add, 0.0)
        inverse = [1.0 / s for s in sums]
        deltas = [jnp.zeros((1, rows), F32) for _ in range(variants)]
        outs = [jnp.zeros((rows, HD), F32) for _ in range(variants)]
        for p, pair in enumerate(pairs):
            prob = scores[p, h] * pick(pair, inverse)
            scores[p, h] = prob
            low = prob.astype(BF16)
            merge(pair, deltas, jnp.sum(prob * prob_grads[p, h], axis=0, keepdims=True), jnp.add, 0.0)
            merge(pair, outs, dot_tn(low, value_of(pair, h)), jnp.add, 0.0)
            term = dot_nn(low, of_variant(pair, grad, h))
            if pair[0] is None:
                own_ref[1, pair[1], :, cols(h)] = term
            else:
                term_ref[slot_of(pair[0]), 1, :, cols(h)] = term.astype(BF16)
        for v in range(variants):
            attended[v, :, cols(h)] = outs[v].astype(BF16)
        dqs = [jnp.zeros((rows, HD), F32) for _ in range(variants)]
        for p, pair in enumerate(pairs):
            ds = (scores[p, h] * (prob_grads[p, h] - pick(pair, deltas)) * scale).astype(BF16)
            merge(pair, dqs, dot_tn(ds, key_of(pair, h)), jnp.add, 0.0)
            term = dot_nn(ds, of_variant(pair, q_ref, h))
            if pair[0] is None:
                own_ref[0, pair[1], :, cols(h)] = term
            else:
                term_ref[slot_of(pair[0]), 0, :, cols(h)] = term.astype(BF16)
        for v in range(variants):
            dq_ref[v, :, cols(h)] = dqs[v].astype(BF16)

    flat = attended[...].reshape(variants * rows, width)
    share = width // RING
    for z in range(RING):
        part = dot_nn(flat, w_ref[:, z * width:(z + 1) * width])
        part_ref[z] = part.astype(BF16).reshape(variants, rows, width)
        block = full_ref[z].reshape(variants * rows, width)
        low = dot_tn(block, flat).astype(BF16)
        for b in range(RING):
            proj_ref[b % 2, z, pl.ds((b // 2) * share, share)] = low[b * share:(b + 1) * share]


def ring_reduce(own, landed, send_sem, recv_sem, me, device_at):
    sides = ((0, -1), (1, 1))
    copies = {}

    def send(side, half, distance):
        step = sides[side][1]
        first = distance == (4 if side == half else 3)
        target = wrap(me + step * distance, RING)
        origin = own.at[target, half] if first else landed.at[side, half, distance]
        copy = pltpu.make_async_remote_copy(
            src_ref=origin,
            dst_ref=landed.at[side, half, distance - 1],
            send_sem=send_sem.at[side, half, distance - 1],
            recv_sem=recv_sem.at[side, half, distance - 1],
            device_id=device_at(wrap(me + step, RING)),
            device_id_type=MESH,
        )
        copy.start()
        copies[side, half, distance] = copy

    def begin():
        for half in range(2):
            for side in range(2):
                start = half if side == 0 else 1 - half
                send(side, start, 4 if side == start else 3)

    def advance(distance, side, half):
        if (side, half, distance) not in copies:
            return
        copies[side, half, distance].wait_recv()
        if distance > 1:
            target = wrap(me + sides[side][1] * (distance - 1), RING)
            here = landed.at[side, half, distance - 1]
            here[...] = (here[...].astype(F32) + own[target, half].astype(F32)).astype(BF16)
            send(side, half, distance - 1)

    def result(half):
        return (
            own[me, half].astype(F32)
            + landed[0, half, 0].astype(F32)
            + landed[1, half, 0].astype(F32)
        )

    def finish():
        for copy in copies.values():
            copy.wait_send()

    return begin, advance, result, finish


CORE_ORDER = (4, 3, -3, 2, -2, 1, -1, 0)


def return_kernel(
    term_ref, part_ref, proj_ref, back_ref, layer_ref, grad_ref,
    layer_land, paired, pair_land, proj_land, row_send_buf, row_land,
    term_send, term_recv, layer_send, layer_recv, pair_send, pair_recv,
    proj_send, proj_recv, row_send, row_recv,
):
    d = lax.axis_index("dp")
    t = lax.axis_index("tensor")
    n_dp = lax.axis_size("dp")
    core = lax.rem(d, 2)
    x = lax.rem(d // 2, ROW)
    y = d // (2 * ROW)

    def at(yy, xx, cc):
        return ((yy * ROW + xx) * 2 + cc, t)

    near = [(wrap(d + o, n_dp), t) for o in OFFSETS]
    beside = [(d, wrap(t + s, RING)) for s in (-1, 1)]
    above = [at(wrap(y + s, RING), x, core) for s in (-1, 1)]
    row = [at(y, lax.rem(x + s, ROW), core) for s in range(1, ROW)]
    greet(near + beside + above + row)

    layer_begin, layer_advance, layer_result, layer_finish = ring_reduce(
        part_ref, layer_land, layer_send, layer_recv, t, lambda z: (d, z)
    )
    layer_begin()

    swaps = []
    for j, r in enumerate(CORE_ORDER):
        chunk = wrap(y + r, RING)
        copy = pltpu.make_async_remote_copy(
            src_ref=proj_ref.at[1 - core, chunk],
            dst_ref=pair_land.at[chunk],
            send_sem=pair_send.at[j],
            recv_sem=pair_recv.at[j],
            device_id=at(y, x, 1 - core),
            device_id_type=MESH,
        )
        copy.start()
        swaps.append(copy)

    terms = []
    for o in FAR_FIRST:
        copy = pltpu.make_async_remote_copy(
            src_ref=term_ref.at[slot_of(o)],
            dst_ref=back_ref.at[slot_of(-o)],
            send_sem=term_send.at[slot_of(o)],
            recv_sem=term_recv.at[slot_of(-o)],
            device_id=(wrap(d + o, n_dp), t),
            device_id_type=MESH,
        )
        copy.start()
        terms.append(copy)

    half_rows = paired.shape[2]
    for j, r in enumerate(CORE_ORDER):
        chunk = wrap(y + r, RING)
        swaps[j].wait_recv()
        for half in range(2):
            span = pl.ds(half * half_rows, half_rows)
            both = proj_ref[core, chunk, span].astype(F32) + pair_land[chunk, span].astype(F32)
            paired[chunk, half] = both.astype(BF16)

    proj_begin, proj_advance, proj_result, proj_finish = ring_reduce(
        paired, proj_land, proj_send, proj_recv, y, lambda yy: at(yy, x, core)
    )
    proj_begin()

    for distance in (4, 3, 2, 1):
        for half in range(2):
            for side in range(2):
                layer_advance(distance, side, half)
                proj_advance(distance, side, half)

    share = row_land.shape[1]
    for half in range(2):
        piece = proj_result(half).astype(BF16)
        for part in range(half_rows // share):
            row_send_buf[half * (half_rows // share) + part] = piece[part * share:(part + 1) * share]
    rows = []
    for s in range(1, ROW):
        xx = lax.rem(x + s, ROW)
        copy = pltpu.make_async_remote_copy(
            src_ref=row_send_buf.at[xx],
            dst_ref=row_land.at[s - 1],
            send_sem=row_send.at[s - 1],
            recv_sem=row_recv.at[s - 1],
            device_id=at(y, xx, core),
            device_id_type=MESH,
        )
        copy.start()
        rows.append(copy)
    for half in range(2):
        layer_ref[half] = layer_result(half).astype(BF16)
    total = row_send_buf[x].astype(F32)
    for s in range(ROW - 1):
        rows[s].wait_recv()
        total = total + row_land[s].astype(F32)
    grad_ref[...] = total
    for copy in rows:
        copy.wait_send()
    for copy in swaps:
        copy.wait_send()
    layer_finish()
    proj_finish()
    for copy in terms:
        copy.wait()


def settle_kernel(
    lists_ref, counts_ref, own_ref, back_ref, layer_in, grad_in, layer_ref, dk_ref, dv_ref, grad_ref
):
    d = lax.axis_index("dp")
    n_dp = lax.axis_size("dp")
    layer_ref[...] = layer_in[...]
    grad_ref[...] = grad_in[...]
    second = [
        lists_block(lists_ref, counts_ref, 1, wrap(d + o, n_dp), d) == 1 for o in OFFSETS
    ]
    for which, out in enumerate((dk_ref, dv_ref)):
        first_sum = own_ref[which, 0]
        second_sum = own_ref[which, 1]
        for o, pick in zip(OFFSETS, second):
            term = back_ref[slot_of(o), which].astype(F32)
            first_sum = first_sum + jnp.where(pick, 0.0, term)
            second_sum = second_sum + jnp.where(pick, term, 0.0)
        out[0] = first_sum.astype(BF16)
        out[1] = second_sum.astype(BF16)


def local(queries, key_rows, value_rows, out_weight, out_grad, ibd_lists, ibd_counts):
    variants, rows, width = queries.shape
    n = len(OFFSETS)
    smem = pl.BlockSpec(memory_space=pltpu.SMEM)
    vmem = pl.BlockSpec(memory_space=VMEM)
    anywhere = pl.BlockSpec(memory_space=pl.ANY)
    dma = pltpu.SemaphoreType.DMA
    shape = jax.ShapeDtypeStruct
    limit = 48 * 1024 * 1024
    share = width // RING

    window, full = pl.pallas_call(
        fetch_kernel,
        out_shape=(
            shape((n, 2, rows, width), BF16),
            shape((RING, variants, rows, width), BF16),
        ),
        in_specs=[smem, smem, vmem, vmem, anywhere],
        out_specs=(anywhere, anywhere),
        scratch_shapes=[
            VMEM((n, 2, rows, width), BF16),
            dma((n,)), dma((n,)), dma((2, 4, 2)), dma((2, 4, 2)), dma,
        ],
        compiler_params=pltpu.CompilerParams(
            collective_id=0, has_side_effects=True, vmem_limit_bytes=limit
        ),
        name="fetch",
    )(ibd_lists, ibd_counts, key_rows, value_rows, out_grad)

    dq, own, term, part, proj = pl.pallas_call(
        attend_kernel,
        out_shape=(
            shape((variants, rows, width), BF16),
            shape((2, variants, rows, width), F32),
            shape((n, 2, rows, width), BF16),
            shape((RING, variants, rows, width), BF16),
            shape((2, RING, ROW * share, width), BF16),
        ),
        in_specs=[smem, smem] + [vmem] * 6,
        out_specs=(vmem,) * 5,
        scratch_shapes=[
            VMEM((variants, rows, width), BF16),
            VMEM((n + variants, width // HD, rows, rows), F32),
            VMEM((n + variants, width // HD, rows, rows), F32),
            VMEM((variants, rows, width), BF16),
        ],
        compiler_params=pltpu.CompilerParams(vmem_limit_bytes=limit),
        name="attend",
    )(ibd_lists, ibd_counts, queries, key_rows, value_rows, out_weight, window, full)

    half_rows = ROW * share // 2
    back, layer, proj_sum = pl.pallas_call(
        return_kernel,
        out_shape=(
            shape((n, 2, rows, width), BF16),
            shape((variants, rows, width), BF16),
            shape((share, width), F32),
        ),
        in_specs=[anywhere, vmem, vmem],
        out_specs=(anywhere, vmem, vmem),
        scratch_shapes=[
            VMEM((2, 2, 4, rows, width), BF16),
            VMEM((RING, 2, half_rows, width), BF16),
            VMEM((RING, ROW * share, width), BF16),
            VMEM((2, 2, 4, half_rows, width), BF16),
            VMEM((ROW, share, width), BF16),
            VMEM((ROW - 1, share, width), BF16),
            dma((n,)), dma((n,)), dma((2, 2, 4)), dma((2, 2, 4)),
            dma((len(CORE_ORDER),)), dma((len(CORE_ORDER),)),
            dma((2, 2, 4)), dma((2, 2, 4)), dma((ROW - 1,)), dma((ROW - 1,)),
        ],
        compiler_params=pltpu.CompilerParams(
            collective_id=1, has_side_effects=True, vmem_limit_bytes=limit
        ),
        name="return",
    )(term, part, proj)

    layer_out, key_grad, value_grad, proj_grad = pl.pallas_call(
        settle_kernel,
        out_shape=(
            shape((variants, rows, width), BF16),
            shape((variants, rows, width), BF16),
            shape((variants, rows, width), BF16),
            shape((share, width), F32),
        ),
        in_specs=[smem, smem] + [vmem] * 4,
        out_specs=(vmem,) * 4,
        compiler_params=pltpu.CompilerParams(vmem_limit_bytes=limit),
        name="settle",
    )(ibd_lists, ibd_counts, own, back, layer, proj_sum)
    return (layer_out, dq, key_grad, value_grad, proj_grad)


def solution(mesh):
    spec = P(None, "dp", "tensor")
    return jax.shard_map(
        local,
        mesh=mesh,
        in_specs=(spec, spec, spec, P("tensor", None), spec, P(), P()),
        out_specs=(spec, spec, spec, spec, P("dp", "tensor")),
        check_vma=False,
    )
```

```python
import functools
import math

import jax
import jax.numpy as jnp
from jax import lax
from jax.experimental import pallas as pl
from jax.experimental.pallas import tpu as pltpu
from jax.sharding import PartitionSpec as P

HD = 128
NEGATIVE = -1e30
RING = 8
ROW = 4
MESH = pl.DeviceIdType.MESH
VMEM = pltpu.VMEM
F32 = jnp.float32
BF16 = jnp.bfloat16

CORE_ORDER = (4, 3, -3, 2, -2, 1, -1, 0)
RING_ORDER = (-4, 4, -3, 3, -2, 2, -1, 1, 0)
SIDES = ((0, -1), (1, 1))
OWN, SIB, NEAR, CROSS, FAR, ODD = (0, 1), 2, (3, 4), (5, 6), (7, 8), 9
PAIRS = 10


def wrap(index, size):
    return lax.rem(index + size, size)


def dot_nn(a, b):
    return lax.dot_general(a, b, (((1,), (0,)), ((), ())), preferred_element_type=F32)


def dot_nt(a, b):
    return lax.dot_general(a, b, (((1,), (1,)), ((), ())), preferred_element_type=F32)


def dot_tn(a, b):
    return lax.dot_general(a, b, (((0,), (0,)), ((), ())), preferred_element_type=F32)


def listed_in(lists_ref, counts_ref, variant, row, block):
    count = counts_ref[variant, row]
    hit = jnp.int32(0)
    for slot in range(lists_ref.shape[0]):
        same = (lists_ref[slot, variant, row] == block) & (count > slot)
        hit = jnp.where(same, 1, hit)
    return hit


def greet(partners):
    barrier = pltpu.get_barrier_semaphore()
    for partner in partners:
        pl.semaphore_signal(barrier, inc=1, device_id=partner, device_id_type=MESH)
    pl.semaphore_wait(barrier, len(partners))


def ring_reduce(own, landed, send_sem, recv_sem, me, device_at):
    sides = ((0, -1), (1, 1))
    copies = {}

    def send(side, half, distance):
        step = sides[side][1]
        first = distance == (4 if side == half else 3)
        target = wrap(me + step * distance, RING)
        origin = own.at[target, half] if first else landed.at[side, half, distance]
        copy = pltpu.make_async_remote_copy(
            src_ref=origin,
            dst_ref=landed.at[side, half, distance - 1],
            send_sem=send_sem.at[side, half, distance - 1],
            recv_sem=recv_sem.at[side, half, distance - 1],
            device_id=device_at(wrap(me + step, RING)),
            device_id_type=MESH,
        )
        copy.start()
        copies[side, half, distance] = copy

    def begin():
        for half in range(2):
            for side in range(2):
                start = half if side == 0 else 1 - half
                send(side, start, 4 if side == start else 3)

    def advance(distance, side, half):
        if (side, half, distance) not in copies:
            return
        copies[side, half, distance].wait_recv()
        if distance > 1:
            target = wrap(me + sides[side][1] * (distance - 1), RING)
            here = landed.at[side, half, distance - 1]
            here[...] = (here[...].astype(F32) + own[target, half].astype(F32)).astype(BF16)
            send(side, half, distance - 1)

    def result(half):
        return (
            own[me, half].astype(F32)
            + landed[0, half, 0].astype(F32)
            + landed[1, half, 0].astype(F32)
        )

    def finish():
        for copy in copies.values():
            copy.wait_send()

    return begin, advance, result, finish


def whole_kernel(
    lists_ref, counts_ref, q_hbm, k_hbm, v_hbm, w_hbm, og_hbm,
    layer_ref, dq_ref, dk_ref, dv_ref, proj_out,
    q_ref, own_kv, w_ref, full, sib_kv, near, far, relay,
    grad_sum, grad, scores, prob_grads, attended,
    part, proj, layer_land, paired, pair_land, proj_land, row_out, row_land,
    own_term, term, sib_term, from_sib, from_far, relay_term, home_term,
    load_sem, ring_send, ring_recv, near_send, near_recv, sib_send, sib_recv, share_send, share_recv,
    far_send, far_recv, back_send, back_recv, home_send, home_recv,
    layer_send, layer_recv, pair_send, pair_recv, proj_send, proj_recv, row_send, row_recv,
):
    d = lax.axis_index("dp")
    t = lax.axis_index("tensor")
    n_dp = lax.axis_size("dp")
    core = lax.rem(d, 2)
    x = lax.rem(d // 2, ROW)
    y = d // (2 * ROW)
    scale = 1.0 / math.sqrt(HD)
    variants, rows, width = q_ref.shape
    heads = width // HD

    def at(yy, xx, cc):
        return ((yy * ROW + xx) * 2 + cc, t)

    def remote(src, dst, send, recv, device):
        copy = pltpu.make_async_remote_copy(
            src_ref=src, dst_ref=dst, send_sem=send, recv_sem=recv,
            device_id=device, device_id_type=MESH,
        )
        copy.start()
        return copy

    sib = d + 1 - 2 * core
    beside = [wrap(d - 2, n_dp), wrap(d + 2, n_dp)]
    odd = wrap(d + 2 * (2 * core - 1) + 1 - 2 * core, n_dp)
    odd_key = wrap(d + 2 * (1 - 2 * core), n_dp)
    odd_side = 1 - core

    loads = [
        pltpu.make_async_copy(k_hbm, own_kv.at[0], load_sem.at[0]),
        pltpu.make_async_copy(v_hbm, own_kv.at[1], load_sem.at[1]),
        pltpu.make_async_copy(q_hbm, q_ref, load_sem.at[2]),
        pltpu.make_async_copy(og_hbm, full.at[t], load_sem.at[3]),
        pltpu.make_async_copy(w_hbm, w_ref, load_sem.at[4]),
    ]
    for copy in loads:
        copy.start()
    greet(
        [(sib, t), (beside[0], t), (beside[1], t), (odd, t)]
        + [(d, wrap(t + s, RING)) for s in (-1, 1)]
        + [at(wrap(y + s, RING), x, core) for s in (-1, 1)]
        + [at(y, lax.rem(x + s, ROW), core) for s in range(1, ROW)]
    )

    hops = {}

    def hop(side, distance, half):
        step = SIDES[side][1]
        source = wrap(t - step * (distance - 1), RING)
        hops[side, distance, half] = remote(
            og_hbm.at[half] if distance == 1 else full.at[source, half],
            full.at[source, half],
            ring_send.at[side, distance - 1, half],
            ring_recv.at[side, distance - 1, half],
            (d, wrap(t + step, RING)),
        )

    def hop_on(distance):
        for half in range(2):
            for side in range(2):
                if (side, distance, half) in hops:
                    hops[side, distance, half].wait_recv()
                    if distance < 3 or (distance == 3 and half == side):
                        hop(side, distance + 1, half)

    for half in range(2):
        for side in range(2):
            hop(side, 1, half)

    near_copies, sib_copies, share_copies, far_copies = {}, {}, {}, {}
    for kv, source in enumerate((k_hbm, v_hbm)):
        for side in range(2):
            near_copies[1 - side, kv] = remote(
                source, near.at[1 - side, core, kv],
                near_send.at[1 - side, kv], near_recv.at[1 - side, kv], (beside[side], t),
            )
        sib_copies[kv] = remote(
            source, sib_kv.at[kv], sib_send.at[kv], sib_recv.at[kv], (sib, t)
        )

    relay_pick = [
        listed_in(lists_ref, counts_ref, 1, beside[1], beside[0]) == 1,
        listed_in(lists_ref, counts_ref, 1, beside[0], beside[1]) == 1,
        listed_in(lists_ref, counts_ref, 1, odd, odd_key) == 1,
    ]

    def pass_on(kv):
        for side in range(2):
            near_copies[side, kv].wait_recv()
            share_copies[side, kv] = remote(
                near.at[side, core, kv], near.at[side, core, kv],
                share_send.at[side, kv], share_recv.at[side, kv], (sib, t),
            )
            relay[side, kv] = jnp.where(
                relay_pick[side], near[side, core, kv, 1], near[side, core, kv, 0]
            )
            far_copies[side, kv] = remote(
                relay.at[side, kv], far.at[side, kv],
                far_send.at[side, kv], far_recv.at[side, kv], (beside[1 - side], t),
            )
        relay[2, kv] = jnp.where(
            relay_pick[2], near[odd_side, core, kv, 1], near[odd_side, core, kv, 0]
        )
        far_copies[2, kv] = remote(
            relay.at[2, kv], far.at[2, kv], far_send.at[2, kv], far_recv.at[2, kv], (odd, t)
        )

    offsets = {
        SIB: 1 - 2 * core, NEAR[0]: -2, NEAR[1]: 2, CROSS[0]: -1 - 2 * core,
        CROSS[1]: 3 - 2 * core, FAR[0]: -4, FAR[1]: 4, ODD: 6 * core - 3,
    }
    which, live = {}, {}
    for p, offset in offsets.items():
        first = listed_in(lists_ref, counts_ref, 0, d, d + offset)
        which[p] = listed_in(lists_ref, counts_ref, 1, d, d + offset)
        live[p] = (first + which[p]) > 0

    def cols(h):
        return slice(h * HD, (h + 1) * HD)

    def pair_kv(p, kv, h):
        if p in OWN:
            return own_kv[kv, p, :, cols(h)]
        if p == SIB:
            first, second = (sib_kv[kv, v, :, cols(h)] for v in range(2))
            return jnp.where(which[p] == 1, second, first)
        if p in NEAR or p in CROSS:
            side, holder = (p - NEAR[0], core) if p in NEAR else (p - CROSS[0], 1 - core)
            first, second = (near[side, holder, kv, v, :, cols(h)] for v in range(2))
            return jnp.where(which[p] == 1, second, first)
        return far[p - FAR[0], kv, :, cols(h)]

    def of_variant(p, ref, h):
        return ref[p if p in OWN else which[p], :, cols(h)]

    def pick(p, stats):
        return stats[p] if p in OWN else jnp.where(which[p] == 1, stats[1], stats[0])

    def merge(p, stats, new, combine, neutral):
        if p in OWN:
            stats[p] = combine(stats[p], new)
        else:
            for v in range(variants):
                stats[v] = combine(stats[v], jnp.where(which[p] == v, new, neutral))

    def per_head(shape, fill):
        return [[jnp.full(shape, fill, F32) for _ in range(variants)] for _ in range(heads)]

    tops = per_head((1, rows), NEGATIVE)

    def score(p):
        for h in range(heads):
            s = dot_nt(pair_kv(p, 0, h), of_variant(p, q_ref, h)) * scale
            if p not in OWN:
                s = jnp.where(live[p], s, NEGATIVE)
            scores[p, h] = s
            merge(p, tops[h], jnp.max(s, axis=0, keepdims=True), jnp.maximum, NEGATIVE)

    def grad_add(distance, first=False):
        sources = [t] if distance == 0 else [wrap(t - distance, RING)]
        if 0 < distance < 4:
            sources.append(wrap(t + distance, RING))
        for source in sources:
            columns = pl.ds(pl.multiple_of(source * width, width), width)
            piece = dot_nt(full[source].reshape(variants * rows, width), w_ref[:, columns])
            grad_sum[...] = piece if first else grad_sum[...] + piece

    for copy in loads:
        copy.wait()
    for p in OWN:
        score(p)
    grad_add(0, first=True)
    pass_on(0)
    hop_on(1)
    sib_copies[0].wait_recv()
    for p in (SIB, *NEAR):
        score(p)
    grad_add(1)
    pass_on(1)
    hop_on(2)
    for side in range(2):
        share_copies[side, 0].wait_recv()
    for p in CROSS:
        score(p)
    grad_add(2)
    hop_on(3)
    for j in range(3):
        far_copies[j, 0].wait_recv()
    for p in (*FAR, ODD):
        score(p)
    sums = per_head((1, rows), 0.0)
    for p in range(PAIRS):
        for h in range(heads):
            e = jnp.exp(scores[p, h] - pick(p, tops[h]))
            scores[p, h] = e
            merge(p, sums[h], jnp.sum(e, axis=0, keepdims=True), jnp.add, 0.0)
    inverse = [[1.0 / s for s in sums[h]] for h in range(heads)]
    sib_copies[1].wait_recv()
    for side in range(2):
        share_copies[side, 1].wait_recv()
    for j in range(3):
        far_copies[j, 1].wait_recv()
    for h in range(heads):
        outs = [jnp.zeros((rows, HD), F32) for _ in range(variants)]
        for p in range(PAIRS):
            prob = scores[p, h] * pick(p, inverse[h])
            scores[p, h] = prob
            merge(p, outs, dot_tn(prob.astype(BF16), pair_kv(p, 1, h)), jnp.add, 0.0)
        for v in range(variants):
            attended[v, :, cols(h)] = outs[v].astype(BF16)

    for r in RING_ORDER[1:]:
        target = wrap(t + r, RING)
        columns = pl.ds(pl.multiple_of(target * width, width), width)
        flat = attended[...].reshape(variants * rows, width)
        part[target] = dot_nn(flat, w_ref[:, columns]).astype(BF16).reshape(variants, rows, width)
    layer_begin, layer_advance, layer_result, layer_finish = ring_reduce(
        part, layer_land, layer_send, layer_recv, t, lambda z: (d, z)
    )
    layer_begin()

    hop_on(4)
    share = width // RING
    half_rows = paired.shape[2]
    swaps = []
    for j, r in enumerate(CORE_ORDER):
        chunk = wrap(y + r, RING)
        flat = attended[...].reshape(variants * rows, width)
        low = dot_tn(full[chunk].reshape(variants * rows, width), flat).astype(BF16)
        for b in range(RING):
            proj[b % 2, chunk, pl.ds((b // 2) * share, share)] = low[b * share:(b + 1) * share]
        swaps.append(remote(
            proj.at[1 - core, chunk], pair_land.at[chunk], pair_send.at[j], pair_recv.at[j], (sib, t)
        ))
    grad_add(3)
    grad_add(4)
    grad[...] = grad_sum[...].astype(BF16).reshape(variants, rows, width)

    back = {}

    def send_back(p, kv):
        if p == SIB:
            slot, target, device = 0, sib_term.at[kv], sib
        elif p in CROSS:
            side = p - CROSS[0]
            slot, target, device = 1 + side, from_sib.at[side, kv], sib
        elif p in FAR:
            side = p - FAR[0]
            slot, target, device = 3 + side, from_far.at[side, kv], beside[side]
        elif p == ODD:
            slot, target, device = 5, from_far.at[2, kv], odd
        else:
            return
        back[slot, kv] = remote(
            term.at[p - SIB, kv], target, back_send.at[slot, kv], back_recv.at[slot, kv], (device, t)
        )

    outward = (*FAR, ODD, *CROSS, SIB, *NEAR, *OWN)
    deltas = per_head((1, rows), 0.0)
    for p in outward:
        for h in range(heads):
            prob = scores[p, h]
            low = prob.astype(BF16)
            gradient = of_variant(p, grad, h)
            dp = dot_nt(pair_kv(p, 1, h), gradient)
            prob_grads[p, h] = dp
            merge(p, deltas[h], jnp.sum(prob * dp, axis=0, keepdims=True), jnp.add, 0.0)
            value = dot_nn(low, gradient)
            if p in OWN:
                own_term[1, p, :, cols(h)] = value
            else:
                term[p - SIB, 1, :, cols(h)] = value.astype(BF16)
        send_back(p, 1)

    def layer_step(distance):
        for half in range(2):
            for side in range(2):
                layer_advance(distance, side, half)

    def proj_step(distance):
        for half in range(2):
            for side in range(2):
                proj_advance(distance, side, half)

    layer_step(4)
    for j, r in enumerate(CORE_ORDER):
        chunk = wrap(y + r, RING)
        swaps[j].wait_recv()
        for half in range(2):
            span = pl.ds(half * half_rows, half_rows)
            both = proj[core, chunk, span].astype(F32) + pair_land[chunk, span].astype(F32)
            paired[chunk, half] = both.astype(BF16)
    proj_begin, proj_advance, proj_result, proj_finish = ring_reduce(
        paired, proj_land, proj_send, proj_recv, y, lambda yy: at(yy, x, core)
    )
    proj_begin()

    dqs = per_head((rows, HD), 0.0)
    for p in outward:
        for h in range(heads):
            ds = (scores[p, h] * (prob_grads[p, h] - pick(p, deltas[h])) * scale).astype(BF16)
            merge(p, dqs[h], dot_tn(ds, pair_kv(p, 0, h)), jnp.add, 0.0)
            value = dot_nn(ds, of_variant(p, q_ref, h))
            if p in OWN:
                own_term[0, p, :, cols(h)] = value
            else:
                term[p - SIB, 0, :, cols(h)] = value.astype(BF16)
        send_back(p, 0)
    for h in range(heads):
        for v in range(variants):
            dq_ref[v, :, cols(h)] = dqs[h][v].astype(BF16)

    home = {}
    sib_pick = [listed_in(lists_ref, counts_ref, 1, sib, b) == 1 for b in beside]
    own_pick = listed_in(lists_ref, counts_ref, 1, sib, d) == 1

    def relay_back(kv):
        for slot in range(1, 6):
            back[slot, kv].wait_recv()
        for side in range(2):
            parts = [
                (which[NEAR[side]] == 1, term[NEAR[side] - SIB, kv]),
                (sib_pick[side], from_sib[side, kv]),
                (relay_pick[side], from_far[side, kv]),
            ]
            extra = from_far[2, kv].astype(F32)
            extra = jnp.where(odd_side == side, extra, 0.0)
            both = [jnp.where(relay_pick[2], 0.0, extra), jnp.where(relay_pick[2], extra, 0.0)]
            for second, value in parts:
                value = value.astype(F32)
                both[0] = both[0] + jnp.where(second, 0.0, value)
                both[1] = both[1] + jnp.where(second, value, 0.0)
            for v in range(variants):
                relay_term[side, kv, v] = both[v].astype(BF16)
            home[side, kv] = remote(
                relay_term.at[side, kv], home_term.at[1 - side, kv],
                home_send.at[side, kv], home_recv.at[1 - side, kv], (beside[side], t),
            )

    relay_back(1)
    layer_step(3)
    proj_step(4)
    relay_back(0)
    proj_step(3)
    layer_step(2)
    proj_step(2)
    layer_step(1)
    proj_step(1)

    for half in range(2):
        piece = proj_result(half).astype(BF16)
        for i in range(half_rows // share):
            row_out[half * (half_rows // share) + i] = piece[i * share:(i + 1) * share]
    row_copies = []
    for s in range(1, ROW):
        xx = lax.rem(x + s, ROW)
        row_copies.append(remote(
            row_out.at[xx], row_land.at[s - 1], row_send.at[s - 1], row_recv.at[s - 1], at(y, xx, core)
        ))
    for half in range(2):
        layer_ref[half] = layer_result(half).astype(BF16)
    for kv, out in ((1, dv_ref), (0, dk_ref)):
        back[0, kv].wait_recv()
        for side in range(2):
            home[1 - side, kv].wait_recv()
        value = sib_term[kv].astype(F32)
        for v in range(variants):
            mine = jnp.where(own_pick, value if v == 1 else 0.0, 0.0 if v == 1 else value)
            total = own_term[kv, v] + mine
            for side in range(2):
                total = total + home_term[side, kv, v].astype(F32)
            out[v] = total.astype(BF16)
    total = row_out[x].astype(F32)
    for s in range(ROW - 1):
        row_copies[s].wait_recv()
        total = total + row_land[s].astype(F32)
    proj_out[...] = total

    for group in (hops, near_copies, sib_copies, share_copies, far_copies, back, home):
        for copy in group.values():
            copy.wait_send()
    for copy in swaps + row_copies:
        copy.wait_send()
    layer_finish()
    proj_finish()


def settle_kernel(*refs):
    count = len(refs) // 2
    for source, target in zip(refs[:count], refs[count:]):
        target[...] = source[...]


def local(queries, key_rows, value_rows, out_weight, out_grad, ibd_lists, ibd_counts):
    variants, rows, width = queries.shape
    heads = width // HD
    share = width // RING
    half_rows = ROW * share // 2
    smem = pl.BlockSpec(memory_space=pltpu.SMEM)
    vmem = pl.BlockSpec(memory_space=VMEM)
    anywhere = pl.BlockSpec(memory_space=pl.ANY)
    dma = pltpu.SemaphoreType.DMA
    block = (rows, width)
    outs = (
        jax.ShapeDtypeStruct((variants, *block), BF16),
        jax.ShapeDtypeStruct((variants, *block), BF16),
        jax.ShapeDtypeStruct((variants, *block), BF16),
        jax.ShapeDtypeStruct((variants, *block), BF16),
        jax.ShapeDtypeStruct((share, width), F32),
    )
    results = pl.pallas_call(
        whole_kernel,
        out_shape=outs,
        in_specs=[smem, smem] + [anywhere] * 5,
        out_specs=(vmem,) * 5,
        scratch_shapes=[
            VMEM((variants, *block), BF16),
            VMEM((2, variants, *block), BF16),
            VMEM(out_weight.shape, BF16),
            VMEM((RING, variants, *block), BF16),
            VMEM((2, variants, *block), BF16),
            VMEM((2, 2, 2, variants, *block), BF16),
            VMEM((3, 2, *block), BF16),
            VMEM((3, 2, *block), BF16),
            VMEM((variants * rows, width), F32),
            VMEM((variants, *block), BF16),
            VMEM((PAIRS, heads, rows, rows), F32),
            VMEM((PAIRS, heads, rows, rows), F32),
            VMEM((variants, *block), BF16),
            VMEM((RING, variants, *block), BF16),
            VMEM((2, RING, ROW * share, width), BF16),
            VMEM((2, 2, 4, *block), BF16),
            VMEM((RING, 2, half_rows, width), BF16),
            VMEM((RING, ROW * share, width), BF16),
            VMEM((2, 2, 4, half_rows, width), BF16),
            VMEM((ROW, share, width), BF16),
            VMEM((ROW - 1, share, width), BF16),
            VMEM((2, variants, *block), F32),
            VMEM((PAIRS - 2, 2, *block), BF16),
            VMEM((2, *block), BF16),
            VMEM((2, 2, *block), BF16),
            VMEM((3, 2, *block), BF16),
            VMEM((2, 2, variants, *block), BF16),
            VMEM((2, 2, variants, *block), BF16),
            dma((5,)),
            dma((2, 4, 2)), dma((2, 4, 2)),
            dma((2, 2)), dma((2, 2)), dma((2,)), dma((2,)), dma((2, 2)), dma((2, 2)),
            dma((3, 2)), dma((3, 2)), dma((6, 2)), dma((6, 2)), dma((2, 2)), dma((2, 2)),
            dma((2, 2, 4)), dma((2, 2, 4)), dma((8,)), dma((8,)),
            dma((2, 2, 4)), dma((2, 2, 4)), dma((ROW - 1,)), dma((ROW - 1,)),
        ],
        compiler_params=pltpu.CompilerParams(
            collective_id=0, has_side_effects=True, vmem_limit_bytes=60 * 1024 * 1024
        ),
        name="whole",
    )(
        jnp.transpose(ibd_lists, (2, 0, 1)), ibd_counts,
        queries, key_rows, value_rows, out_weight, out_grad,
    )
    return pl.pallas_call(
        settle_kernel,
        out_shape=outs,
        in_specs=[vmem] * 5,
        out_specs=(vmem,) * 5,
        name="settle",
    )(*results)


def solution(mesh):
    spec = P(None, "dp", "tensor")
    return jax.shard_map(
        local,
        mesh=mesh,
        in_specs=(spec, spec, spec, P("tensor", None), spec, P(), P()),
        out_specs=(spec, spec, spec, spec, P("dp", "tensor")),
        check_vma=False,
    )
```

```python
import functools
import math

import jax
import jax.numpy as jnp
from jax import lax
from jax.experimental import pallas as pl
from jax.experimental.pallas import tpu as pltpu
from jax.sharding import PartitionSpec as P

HD = 128
NEGATIVE = -1e30
RING = 8
ROW = 4
MESH = pl.DeviceIdType.MESH
VMEM = pltpu.VMEM
F32 = jnp.float32
BF16 = jnp.bfloat16

CORE_ORDER = (4, 3, -3, 2, -2, 1, -1, 0)
SIDES = ((0, -1), (1, 1))
OWN, SIB, NEAR, CROSS, FAR, ODD = (0, 1), 2, (3, 4), (5, 6), (7, 8), 9
PAIRS = 10


def wrap(index, size):
    return lax.rem(index + size, size)


def dot_nn(a, b):
    return lax.dot_general(a, b, (((1,), (0,)), ((), ())), preferred_element_type=F32)


def dot_nt(a, b):
    return lax.dot_general(a, b, (((1,), (1,)), ((), ())), preferred_element_type=F32)


def dot_tn(a, b):
    return lax.dot_general(a, b, (((0,), (0,)), ((), ())), preferred_element_type=F32)


def listed_in(lists_ref, counts_ref, variant, row, block):
    count = counts_ref[variant, row]
    hit = jnp.int32(0)
    for slot in range(lists_ref.shape[0]):
        same = (lists_ref[slot, variant, row] == block) & (count > slot)
        hit = jnp.where(same, 1, hit)
    return hit


def greet(partners):
    barrier = pltpu.get_barrier_semaphore()
    for partner in partners:
        pl.semaphore_signal(barrier, inc=1, device_id=partner, device_id_type=MESH)
    pl.semaphore_wait(barrier, len(partners))


def ring_reduce(own, landed, send_sem, recv_sem, me, device_at):
    sides = ((0, -1), (1, 1))
    copies = {}

    def send(side, half, distance):
        step = sides[side][1]
        first = distance == (4 if side == half else 3)
        target = wrap(me + step * distance, RING)
        origin = own.at[target, half] if first else landed.at[side, half, distance]
        copy = pltpu.make_async_remote_copy(
            src_ref=origin,
            dst_ref=landed.at[side, half, distance - 1],
            send_sem=send_sem.at[side, half, distance - 1],
            recv_sem=recv_sem.at[side, half, distance - 1],
            device_id=device_at(wrap(me + step, RING)),
            device_id_type=MESH,
        )
        copy.start()
        copies[side, half, distance] = copy

    def begin(distance):
        for side in range(2):
            send(side, side if distance == 4 else 1 - side, distance)

    def advance(distance, side, half):
        if (side, half, distance) not in copies:
            return
        copies[side, half, distance].wait_recv()
        if distance > 1:
            target = wrap(me + sides[side][1] * (distance - 1), RING)
            here = landed.at[side, half, distance - 1]
            here[...] = (here[...].astype(F32) + own[target, half].astype(F32)).astype(BF16)
            send(side, half, distance - 1)

    def result(half):
        return (
            own[me, half].astype(F32)
            + landed[0, half, 0].astype(F32)
            + landed[1, half, 0].astype(F32)
        )

    def finish():
        for copy in copies.values():
            copy.wait_send()

    return begin, advance, result, finish


def whole_kernel(
    lists_ref, counts_ref, q_hbm, k_hbm, v_hbm, w_hbm, og_hbm,
    layer_ref, dq_ref, dk_ref, dv_ref, proj_out,
    q_ref, own_kv, w_ref, full, sib_kv, near, far, relay,
    grad_sum, grad, scores, prob_grads, attended,
    part, proj, layer_land, paired, pair_land, proj_land, row_out, row_land,
    own_term, term, sib_term, from_sib, from_far, relay_term, home_term,
    load_sem, ring_send, ring_recv, near_send, near_recv, sib_send, sib_recv, share_send, share_recv,
    far_send, far_recv, back_send, back_recv, home_send, home_recv,
    layer_send, layer_recv, pair_send, pair_recv, proj_send, proj_recv, row_send, row_recv,
):
    d = lax.axis_index("dp")
    t = lax.axis_index("tensor")
    n_dp = lax.axis_size("dp")
    core = lax.rem(d, 2)
    x = lax.rem(d // 2, ROW)
    y = d // (2 * ROW)
    scale = 1.0 / math.sqrt(HD)
    variants, rows, width = q_ref.shape
    heads = width // HD

    def at(yy, xx, cc):
        return ((yy * ROW + xx) * 2 + cc, t)

    def remote(src, dst, send, recv, device):
        copy = pltpu.make_async_remote_copy(
            src_ref=src, dst_ref=dst, send_sem=send, recv_sem=recv,
            device_id=device, device_id_type=MESH,
        )
        copy.start()
        return copy

    sib = d + 1 - 2 * core
    beside = [wrap(d - 2, n_dp), wrap(d + 2, n_dp)]
    odd = wrap(d + 2 * (2 * core - 1) + 1 - 2 * core, n_dp)
    odd_key = wrap(d + 2 * (1 - 2 * core), n_dp)
    odd_side = 1 - core

    loads = [
        pltpu.make_async_copy(k_hbm, own_kv.at[0], load_sem.at[0]),
        pltpu.make_async_copy(v_hbm, own_kv.at[1], load_sem.at[1]),
        pltpu.make_async_copy(q_hbm, q_ref, load_sem.at[2]),
        pltpu.make_async_copy(og_hbm, full.at[t], load_sem.at[3]),
        pltpu.make_async_copy(w_hbm, w_ref, load_sem.at[4]),
    ]
    for copy in loads:
        copy.start()
    greet(
        [(sib, t), (beside[0], t), (beside[1], t), (odd, t)]
        + [(d, wrap(t + s, RING)) for s in (-1, 1)]
        + [at(wrap(y + s, RING), x, core) for s in (-1, 1)]
        + [at(y, lax.rem(x + s, ROW), core) for s in range(1, ROW)]
    )

    hops = {}

    def hop(side, distance, half):
        step = SIDES[side][1]
        source = wrap(t - step * (distance - 1), RING)
        hops[side, distance, half] = remote(
            og_hbm.at[half] if distance == 1 else full.at[source, half],
            full.at[source, half],
            ring_send.at[side, distance - 1, half],
            ring_recv.at[side, distance - 1, half],
            (d, wrap(t + step, RING)),
        )

    def hop_on(distance):
        for half in range(2):
            for side in range(2):
                if (side, distance, half) in hops:
                    hops[side, distance, half].wait_recv()
                    if distance < 3 or (distance == 3 and half == side):
                        hop(side, distance + 1, half)

    for half in range(2):
        for side in range(2):
            hop(side, 1, half)

    near_copies, sib_copies, share_copies, far_copies = {}, {}, {}, {}
    for kv, source in enumerate((k_hbm, v_hbm)):
        for side in range(2):
            near_copies[1 - side, kv] = remote(
                source, near.at[1 - side, core, kv],
                near_send.at[1 - side, kv], near_recv.at[1 - side, kv], (beside[side], t),
            )
        sib_copies[kv] = remote(
            source, sib_kv.at[kv], sib_send.at[kv], sib_recv.at[kv], (sib, t)
        )

    relay_pick = [
        listed_in(lists_ref, counts_ref, 1, beside[1], beside[0]) == 1,
        listed_in(lists_ref, counts_ref, 1, beside[0], beside[1]) == 1,
        listed_in(lists_ref, counts_ref, 1, odd, odd_key) == 1,
    ]

    def pass_on(kv):
        for side in range(2):
            near_copies[side, kv].wait_recv()
            share_copies[side, kv] = remote(
                near.at[side, core, kv], near.at[side, core, kv],
                share_send.at[side, kv], share_recv.at[side, kv], (sib, t),
            )
            relay[side, kv] = jnp.where(
                relay_pick[side], near[side, core, kv, 1], near[side, core, kv, 0]
            )
            far_copies[side, kv] = remote(
                relay.at[side, kv], far.at[side, kv],
                far_send.at[side, kv], far_recv.at[side, kv], (beside[1 - side], t),
            )
        relay[2, kv] = jnp.where(
            relay_pick[2], near[odd_side, core, kv, 1], near[odd_side, core, kv, 0]
        )
        far_copies[2, kv] = remote(
            relay.at[2, kv], far.at[2, kv], far_send.at[2, kv], far_recv.at[2, kv], (odd, t)
        )

    offsets = {
        SIB: 1 - 2 * core, NEAR[0]: -2, NEAR[1]: 2, CROSS[0]: -1 - 2 * core,
        CROSS[1]: 3 - 2 * core, FAR[0]: -4, FAR[1]: 4, ODD: 6 * core - 3,
    }
    which, live = {}, {}
    for p, offset in offsets.items():
        first = listed_in(lists_ref, counts_ref, 0, d, d + offset)
        which[p] = listed_in(lists_ref, counts_ref, 1, d, d + offset)
        live[p] = (first + which[p]) > 0

    def cols(h):
        return slice(h * HD, (h + 1) * HD)

    def pair_kv(p, kv, h):
        if p in OWN:
            return own_kv[kv, p, :, cols(h)]
        if p == SIB:
            first, second = (sib_kv[kv, v, :, cols(h)] for v in range(2))
            return jnp.where(which[p] == 1, second, first)
        if p in NEAR or p in CROSS:
            side, holder = (p - NEAR[0], core) if p in NEAR else (p - CROSS[0], 1 - core)
            first, second = (near[side, holder, kv, v, :, cols(h)] for v in range(2))
            return jnp.where(which[p] == 1, second, first)
        return far[p - FAR[0], kv, :, cols(h)]

    def of_variant(p, ref, h):
        return ref[p if p in OWN else which[p], :, cols(h)]

    def pick(p, stats):
        return stats[p] if p in OWN else jnp.where(which[p] == 1, stats[1], stats[0])

    def merge(p, stats, new, combine, neutral):
        if p in OWN:
            stats[p] = combine(stats[p], new)
        else:
            for v in range(variants):
                stats[v] = combine(stats[v], jnp.where(which[p] == v, new, neutral))

    def per_head(shape, fill):
        return [[jnp.full(shape, fill, F32) for _ in range(variants)] for _ in range(heads)]

    tops = per_head((1, rows), NEGATIVE)

    def score(p):
        for h in range(heads):
            s = dot_nt(pair_kv(p, 0, h), of_variant(p, q_ref, h)) * scale
            if p not in OWN:
                s = jnp.where(live[p], s, NEGATIVE)
            scores[p, h] = s
            merge(p, tops[h], jnp.max(s, axis=0, keepdims=True), jnp.maximum, NEGATIVE)

    def grad_add(distance, first=False):
        sources = [t] if distance == 0 else [wrap(t - distance, RING)]
        if 0 < distance < 4:
            sources.append(wrap(t + distance, RING))
        for source in sources:
            columns = pl.ds(pl.multiple_of(source * width, width), width)
            piece = dot_nt(full[source].reshape(variants * rows, width), w_ref[:, columns])
            grad_sum[...] = piece if first else grad_sum[...] + piece

    for copy in loads:
        copy.wait()
    for p in OWN:
        score(p)
    grad_add(0, first=True)
    pass_on(0)
    hop_on(1)
    sib_copies[0].wait_recv()
    for p in (SIB, *NEAR):
        score(p)
    grad_add(1)
    pass_on(1)
    hop_on(2)
    for side in range(2):
        share_copies[side, 0].wait_recv()
    for p in CROSS:
        score(p)
    grad_add(2)
    hop_on(3)
    grad_add(3)
    for j in range(3):
        far_copies[j, 0].wait_recv()
    for p in (*FAR, ODD):
        score(p)
    sums = per_head((1, rows), 0.0)
    for p in range(PAIRS):
        for h in range(heads):
            e = jnp.exp(scores[p, h] - pick(p, tops[h]))
            scores[p, h] = e
            merge(p, sums[h], jnp.sum(e, axis=0, keepdims=True), jnp.add, 0.0)
    inverse = [[1.0 / s for s in sums[h]] for h in range(heads)]
    sib_copies[1].wait_recv()
    for side in range(2):
        share_copies[side, 1].wait_recv()
    for j in range(3):
        far_copies[j, 1].wait_recv()
    for h in range(heads):
        outs = [jnp.zeros((rows, HD), F32) for _ in range(variants)]
        for p in range(PAIRS):
            prob = scores[p, h] * pick(p, inverse[h])
            scores[p, h] = prob
            merge(p, outs, dot_tn(prob.astype(BF16), pair_kv(p, 1, h)), jnp.add, 0.0)
        for v in range(variants):
            attended[v, :, cols(h)] = outs[v].astype(BF16)

    layer_begin, layer_advance, layer_result, layer_finish = ring_reduce(
        part, layer_land, layer_send, layer_recv, t, lambda z: (d, z)
    )
    for r in CORE_ORDER:
        target = wrap(t + r, RING)
        columns = pl.ds(pl.multiple_of(target * width, width), width)
        flat = attended[...].reshape(variants * rows, width)
        part[target] = dot_nn(flat, w_ref[:, columns]).astype(BF16).reshape(variants, rows, width)
        if r in (4, -3):
            layer_begin(abs(r))

    hop_on(4)
    share = width // RING
    half_rows = paired.shape[2]
    swaps = {}
    for j, r in enumerate(CORE_ORDER):
        chunk = wrap(y + r, RING)
        flat = attended[...].reshape(variants * rows, width)
        low = dot_tn(full[chunk].reshape(variants * rows, width), flat).astype(BF16)
        for b in range(RING):
            proj[b % 2, chunk, pl.ds((b // 2) * share, share)] = low[b * share:(b + 1) * share]
        swaps[r] = remote(
            proj.at[1 - core, chunk], pair_land.at[chunk], pair_send.at[j], pair_recv.at[j], (sib, t)
        )
    proj_begin, proj_advance, proj_result, proj_finish = ring_reduce(
        paired, proj_land, proj_send, proj_recv, y, lambda yy: at(yy, x, core)
    )

    def pair_up(*chunks):
        for r in chunks:
            chunk = wrap(y + r, RING)
            swaps[r].wait_recv()
            for half in range(2):
                span = pl.ds(half * half_rows, half_rows)
                both = proj[core, chunk, span].astype(F32) + pair_land[chunk, span].astype(F32)
                paired[chunk, half] = both.astype(BF16)

    def layer_step(distance):
        for half in range(2):
            for side in range(2):
                layer_advance(distance, side, half)

    def proj_step(distance):
        for half in range(2):
            for side in range(2):
                proj_advance(distance, side, half)

    grad_add(4)
    grad[...] = grad_sum[...].astype(BF16).reshape(variants, rows, width)

    back = {}

    def send_back(p, kv):
        if p == SIB:
            slot, target, device = 0, sib_term.at[kv], sib
        elif p in CROSS:
            side = p - CROSS[0]
            slot, target, device = 1 + side, from_sib.at[side, kv], sib
        elif p in FAR:
            side = p - FAR[0]
            slot, target, device = 3 + side, from_far.at[side, kv], beside[side]
        elif p == ODD:
            slot, target, device = 5, from_far.at[2, kv], odd
        else:
            return
        back[slot, kv] = remote(
            term.at[p - SIB, kv], target, back_send.at[slot, kv], back_recv.at[slot, kv], (device, t)
        )

    deltas = per_head((1, rows), 0.0)

    def value_terms(*which_pairs):
        for p in which_pairs:
            for h in range(heads):
                prob = scores[p, h]
                low = prob.astype(BF16)
                gradient = of_variant(p, grad, h)
                dp = dot_nt(pair_kv(p, 1, h), gradient)
                prob_grads[p, h] = dp
                merge(p, deltas[h], jnp.sum(prob * dp, axis=0, keepdims=True), jnp.add, 0.0)
                value = dot_nn(low, gradient)
                if p in OWN:
                    own_term[1, p, :, cols(h)] = value
                else:
                    term[p - SIB, 1, :, cols(h)] = value.astype(BF16)
            send_back(p, 1)

    dqs = per_head((rows, HD), 0.0)

    def key_terms(*which_pairs):
        for p in which_pairs:
            for h in range(heads):
                ds = (scores[p, h] * (prob_grads[p, h] - pick(p, deltas[h])) * scale).astype(BF16)
                merge(p, dqs[h], dot_tn(ds, pair_kv(p, 0, h)), jnp.add, 0.0)
                value = dot_nn(ds, of_variant(p, q_ref, h))
                if p in OWN:
                    own_term[0, p, :, cols(h)] = value
                else:
                    term[p - SIB, 0, :, cols(h)] = value.astype(BF16)
            send_back(p, 0)

    home = {}
    sib_pick = [listed_in(lists_ref, counts_ref, 1, sib, b) == 1 for b in beside]
    own_pick = listed_in(lists_ref, counts_ref, 1, sib, d) == 1

    def relay_back(kv):
        for slot in range(1, 6):
            back[slot, kv].wait_recv()
        for side in range(2):
            parts = [
                (which[NEAR[side]] == 1, term[NEAR[side] - SIB, kv]),
                (sib_pick[side], from_sib[side, kv]),
                (relay_pick[side], from_far[side, kv]),
            ]
            extra = from_far[2, kv].astype(F32)
            extra = jnp.where(odd_side == side, extra, 0.0)
            both = [jnp.where(relay_pick[2], 0.0, extra), jnp.where(relay_pick[2], extra, 0.0)]
            for second, value in parts:
                value = value.astype(F32)
                both[0] = both[0] + jnp.where(second, 0.0, value)
                both[1] = both[1] + jnp.where(second, value, 0.0)
            for v in range(variants):
                relay_term[side, kv, v] = both[v].astype(BF16)
            home[side, kv] = remote(
                relay_term.at[side, kv], home_term.at[1 - side, kv],
                home_send.at[side, kv], home_recv.at[1 - side, kv], (beside[side], t),
            )

    value_terms(*FAR, ODD, *CROSS)
    pair_up(4)
    proj_begin(4)
    pair_up(3, -3)
    proj_begin(3)
    value_terms(SIB, *NEAR, *OWN)
    layer_step(4)
    key_terms(*FAR, ODD, *CROSS)
    pair_up(2, -2)
    proj_step(4)
    relay_back(1)
    pair_up(1, -1, 0)
    proj_step(3)
    layer_step(3)
    key_terms(SIB, *NEAR, *OWN)
    for h in range(heads):
        for v in range(variants):
            dq_ref[v, :, cols(h)] = dqs[h][v].astype(BF16)
    relay_back(0)
    proj_step(2)
    layer_step(2)
    proj_step(1)

    for half in range(2):
        piece = proj_result(half).astype(BF16)
        for i in range(half_rows // share):
            row_out[half * (half_rows // share) + i] = piece[i * share:(i + 1) * share]
    row_copies = []
    for s in range(1, ROW):
        xx = lax.rem(x + s, ROW)
        row_copies.append(remote(
            row_out.at[xx], row_land.at[s - 1], row_send.at[s - 1], row_recv.at[s - 1], at(y, xx, core)
        ))
    layer_step(1)
    for half in range(2):
        layer_ref[half] = layer_result(half).astype(BF16)
    for kv, out in ((1, dv_ref), (0, dk_ref)):
        back[0, kv].wait_recv()
        for side in range(2):
            home[1 - side, kv].wait_recv()
        value = sib_term[kv].astype(F32)
        for v in range(variants):
            mine = jnp.where(own_pick, value if v == 1 else 0.0, 0.0 if v == 1 else value)
            total = own_term[kv, v] + mine
            for side in range(2):
                total = total + home_term[side, kv, v].astype(F32)
            out[v] = total.astype(BF16)
    total = row_out[x].astype(F32)
    for s in range(ROW - 1):
        row_copies[s].wait_recv()
        total = total + row_land[s].astype(F32)
    proj_out[...] = total

    for group in (hops, near_copies, sib_copies, share_copies, far_copies, back, home):
        for copy in group.values():
            copy.wait_send()
    for copy in [*swaps.values(), *row_copies]:
        copy.wait_send()
    layer_finish()
    proj_finish()


def settle_kernel(*refs):
    count = len(refs) // 2
    for source, target in zip(refs[:count], refs[count:]):
        target[...] = source[...]


def local(queries, key_rows, value_rows, out_weight, out_grad, ibd_lists, ibd_counts):
    variants, rows, width = queries.shape
    heads = width // HD
    share = width // RING
    half_rows = ROW * share // 2
    smem = pl.BlockSpec(memory_space=pltpu.SMEM)
    vmem = pl.BlockSpec(memory_space=VMEM)
    anywhere = pl.BlockSpec(memory_space=pl.ANY)
    dma = pltpu.SemaphoreType.DMA
    block = (rows, width)
    outs = (
        jax.ShapeDtypeStruct((variants, *block), BF16),
        jax.ShapeDtypeStruct((variants, *block), BF16),
        jax.ShapeDtypeStruct((variants, *block), BF16),
        jax.ShapeDtypeStruct((variants, *block), BF16),
        jax.ShapeDtypeStruct((share, width), F32),
    )
    results = pl.pallas_call(
        whole_kernel,
        out_shape=outs,
        in_specs=[smem, smem] + [anywhere] * 5,
        out_specs=(vmem,) * 5,
        scratch_shapes=[
            VMEM((variants, *block), BF16),
            VMEM((2, variants, *block), BF16),
            VMEM(out_weight.shape, BF16),
            VMEM((RING, variants, *block), BF16),
            VMEM((2, variants, *block), BF16),
            VMEM((2, 2, 2, variants, *block), BF16),
            VMEM((3, 2, *block), BF16),
            VMEM((3, 2, *block), BF16),
            VMEM((variants * rows, width), F32),
            VMEM((variants, *block), BF16),
            VMEM((PAIRS, heads, rows, rows), F32),
            VMEM((PAIRS, heads, rows, rows), F32),
            VMEM((variants, *block), BF16),
            VMEM((RING, variants, *block), BF16),
            VMEM((2, RING, ROW * share, width), BF16),
            VMEM((2, 2, 4, *block), BF16),
            VMEM((RING, 2, half_rows, width), BF16),
            VMEM((RING, ROW * share, width), BF16),
            VMEM((2, 2, 4, half_rows, width), BF16),
            VMEM((ROW, share, width), BF16),
            VMEM((ROW - 1, share, width), BF16),
            VMEM((2, variants, *block), F32),
            VMEM((PAIRS - 2, 2, *block), BF16),
            VMEM((2, *block), BF16),
            VMEM((2, 2, *block), BF16),
            VMEM((3, 2, *block), BF16),
            VMEM((2, 2, variants, *block), BF16),
            VMEM((2, 2, variants, *block), BF16),
            dma((5,)),
            dma((2, 4, 2)), dma((2, 4, 2)),
            dma((2, 2)), dma((2, 2)), dma((2,)), dma((2,)), dma((2, 2)), dma((2, 2)),
            dma((3, 2)), dma((3, 2)), dma((6, 2)), dma((6, 2)), dma((2, 2)), dma((2, 2)),
            dma((2, 2, 4)), dma((2, 2, 4)), dma((8,)), dma((8,)),
            dma((2, 2, 4)), dma((2, 2, 4)), dma((ROW - 1,)), dma((ROW - 1,)),
        ],
        compiler_params=pltpu.CompilerParams(
            collective_id=0, has_side_effects=True, vmem_limit_bytes=60 * 1024 * 1024
        ),
        name="whole",
    )(
        jnp.transpose(ibd_lists, (2, 0, 1)), ibd_counts,
        queries, key_rows, value_rows, out_weight, out_grad,
    )
    return pl.pallas_call(
        settle_kernel,
        out_shape=outs,
        in_specs=[vmem] * 5,
        out_specs=(vmem,) * 5,
        name="settle",
    )(*results)


def solution(mesh):
    spec = P(None, "dp", "tensor")
    return jax.shard_map(
        local,
        mesh=mesh,
        in_specs=(spec, spec, spec, P("tensor", None), spec, P(), P()),
        out_specs=(spec, spec, spec, spec, P("dp", "tensor")),
        check_vma=False,
    )
```

```python
import functools
import math

import jax
import jax.numpy as jnp
from jax import lax
from jax.experimental import pallas as pl
from jax.experimental.pallas import tpu as pltpu
from jax.sharding import PartitionSpec as P

HD = 128
NEGATIVE = -1e30
RING = 8
ROW = 4
MESH = pl.DeviceIdType.MESH
VMEM = pltpu.VMEM
F32 = jnp.float32
BF16 = jnp.bfloat16

CORE_ORDER = (4, 3, -3, 2, -2, 1, -1, 0)
SIDES = ((0, -1), (1, 1))
OWN, SIB, NEAR, CROSS, FAR, ODD = (0, 1), 2, (3, 4), (5, 6), (7, 8), 9
PAIRS = 10


def wrap(index, size):
    return lax.rem(index + size, size)


def dot_nn(a, b):
    return lax.dot_general(a, b, (((1,), (0,)), ((), ())), preferred_element_type=F32)


def dot_nt(a, b):
    return lax.dot_general(a, b, (((1,), (1,)), ((), ())), preferred_element_type=F32)


def dot_tn(a, b):
    return lax.dot_general(a, b, (((0,), (0,)), ((), ())), preferred_element_type=F32)


def listed_in(lists_ref, counts_ref, variant, row, block):
    count = counts_ref[variant, row]
    hit = jnp.int32(0)
    for slot in range(lists_ref.shape[0]):
        same = (lists_ref[slot, variant, row] == block) & (count > slot)
        hit = jnp.where(same, 1, hit)
    return hit


def greet(partners):
    barrier = pltpu.get_barrier_semaphore()
    for partner in partners:
        pl.semaphore_signal(barrier, inc=1, device_id=partner, device_id_type=MESH)
    pl.semaphore_wait(barrier, len(partners))


def ring_reduce(own, landed, send_sem, recv_sem, me, device_at):
    sides = ((0, -1), (1, 1))
    copies = {}

    def send(side, half, distance):
        step = sides[side][1]
        first = distance == (4 if side == half else 3)
        target = wrap(me + step * distance, RING)
        origin = own.at[target, half] if first else landed.at[side, half, distance]
        copy = pltpu.make_async_remote_copy(
            src_ref=origin,
            dst_ref=landed.at[side, half, distance - 1],
            send_sem=send_sem.at[side, half, distance - 1],
            recv_sem=recv_sem.at[side, half, distance - 1],
            device_id=device_at(wrap(me + step, RING)),
            device_id_type=MESH,
        )
        copy.start()
        copies[side, half, distance] = copy

    def begin(distance):
        for side in range(2):
            send(side, side if distance == 4 else 1 - side, distance)

    def advance(distance, side, half):
        if (side, half, distance) not in copies:
            return
        copies[side, half, distance].wait_recv()
        if distance > 1:
            target = wrap(me + sides[side][1] * (distance - 1), RING)
            here = landed.at[side, half, distance - 1]
            here[...] = (here[...].astype(F32) + own[target, half].astype(F32)).astype(BF16)
            send(side, half, distance - 1)

    def result(half):
        return (
            own[me, half].astype(F32)
            + landed[0, half, 0].astype(F32)
            + landed[1, half, 0].astype(F32)
        )

    def finish():
        for copy in copies.values():
            copy.wait_send()

    return begin, advance, result, finish


def whole_kernel(
    lists_ref, counts_ref, q_hbm, k_hbm, v_hbm, w_hbm, og_hbm,
    layer_ref, dq_ref, dk_ref, dv_ref, proj_out,
    q_ref, own_kv, w_ref, full, sib_kv, near, far, relay,
    grad_sum, grad, scores, prob_grads, attended,
    part, proj, layer_land, paired, pair_land, proj_land, row_out, row_land,
    own_term, term, sib_term, from_sib, from_far, relay_term, home_term,
    load_sem, ring_send, ring_recv, near_send, near_recv, sib_send, sib_recv, share_send, share_recv,
    far_send, far_recv, back_send, back_recv, home_send, home_recv,
    layer_send, layer_recv, pair_send, pair_recv, proj_send, proj_recv, row_send, row_recv,
):
    d = lax.axis_index("dp")
    t = lax.axis_index("tensor")
    n_dp = lax.axis_size("dp")
    core = lax.rem(d, 2)
    x = lax.rem(d // 2, ROW)
    y = d // (2 * ROW)
    scale = 1.0 / math.sqrt(HD)
    variants, rows, width = q_ref.shape
    heads = width // HD

    def at(yy, xx, cc):
        return ((yy * ROW + xx) * 2 + cc, t)

    def remote(src, dst, send, recv, device):
        copy = pltpu.make_async_remote_copy(
            src_ref=src, dst_ref=dst, send_sem=send, recv_sem=recv,
            device_id=device, device_id_type=MESH,
        )
        copy.start()
        return copy

    sib = d + 1 - 2 * core
    beside = [wrap(d - 2, n_dp), wrap(d + 2, n_dp)]
    odd = wrap(d + 2 * (2 * core - 1) + 1 - 2 * core, n_dp)
    odd_key = wrap(d + 2 * (1 - 2 * core), n_dp)
    odd_side = 1 - core

    loads = [
        pltpu.make_async_copy(k_hbm, own_kv.at[0], load_sem.at[0]),
        pltpu.make_async_copy(v_hbm, own_kv.at[1], load_sem.at[1]),
        pltpu.make_async_copy(q_hbm, q_ref, load_sem.at[2]),
        pltpu.make_async_copy(og_hbm, full.at[t], load_sem.at[3]),
        pltpu.make_async_copy(w_hbm, w_ref, load_sem.at[4]),
    ]
    for copy in loads:
        copy.start()
    greet(
        [(sib, t), (beside[0], t), (beside[1], t), (odd, t)]
        + [(d, wrap(t + s, RING)) for s in (-1, 1)]
        + [at(wrap(y + s, RING), x, core) for s in (-1, 1)]
        + [at(y, lax.rem(x + s, ROW), core) for s in range(1, ROW)]
    )

    hops = {}

    def hop(side, distance, half):
        step = SIDES[side][1]
        source = wrap(t - step * (distance - 1), RING)
        hops[side, distance, half] = remote(
            og_hbm.at[half] if distance == 1 else full.at[source, half],
            full.at[source, half],
            ring_send.at[side, distance - 1, half],
            ring_recv.at[side, distance - 1, half],
            (d, wrap(t + step, RING)),
        )

    def hop_on(distance, *halves):
        for half in halves:
            for side in range(2):
                if (side, distance, half) in hops:
                    hops[side, distance, half].wait_recv()
                    if distance < 3 or (distance == 3 and half == side):
                        hop(side, distance + 1, half)

    for half in range(2):
        for side in range(2):
            hop(side, 1, half)

    near_copies, sib_copies, share_copies, far_copies = {}, {}, {}, {}
    for kv, source in enumerate((k_hbm, v_hbm)):
        for side in range(2):
            near_copies[1 - side, kv] = remote(
                source, near.at[1 - side, core, kv],
                near_send.at[1 - side, kv], near_recv.at[1 - side, kv], (beside[side], t),
            )
        sib_copies[kv] = remote(
            source, sib_kv.at[kv], sib_send.at[kv], sib_recv.at[kv], (sib, t)
        )

    relay_pick = [
        listed_in(lists_ref, counts_ref, 1, beside[1], beside[0]) == 1,
        listed_in(lists_ref, counts_ref, 1, beside[0], beside[1]) == 1,
        listed_in(lists_ref, counts_ref, 1, odd, odd_key) == 1,
    ]

    def pass_on(kv):
        for side in range(2):
            near_copies[side, kv].wait_recv()
            share_copies[side, kv] = remote(
                near.at[side, core, kv], near.at[side, core, kv],
                share_send.at[side, kv], share_recv.at[side, kv], (sib, t),
            )
            relay[side, kv] = jnp.where(
                relay_pick[side], near[side, core, kv, 1], near[side, core, kv, 0]
            )
            far_copies[side, kv] = remote(
                relay.at[side, kv], far.at[side, kv],
                far_send.at[side, kv], far_recv.at[side, kv], (beside[1 - side], t),
            )
        relay[2, kv] = jnp.where(
            relay_pick[2], near[odd_side, core, kv, 1], near[odd_side, core, kv, 0]
        )
        far_copies[2, kv] = remote(
            relay.at[2, kv], far.at[2, kv], far_send.at[2, kv], far_recv.at[2, kv], (odd, t)
        )

    offsets = {
        SIB: 1 - 2 * core, NEAR[0]: -2, NEAR[1]: 2, CROSS[0]: -1 - 2 * core,
        CROSS[1]: 3 - 2 * core, FAR[0]: -4, FAR[1]: 4, ODD: 6 * core - 3,
    }
    which, live = {}, {}
    for p, offset in offsets.items():
        first = listed_in(lists_ref, counts_ref, 0, d, d + offset)
        which[p] = listed_in(lists_ref, counts_ref, 1, d, d + offset)
        live[p] = (first + which[p]) > 0

    def cols(h):
        return slice(h * HD, (h + 1) * HD)

    def pair_kv(p, kv, h):
        if p in OWN:
            return own_kv[kv, p, :, cols(h)]
        if p == SIB:
            first, second = (sib_kv[kv, v, :, cols(h)] for v in range(2))
            return jnp.where(which[p] == 1, second, first)
        if p in NEAR or p in CROSS:
            side, holder = (p - NEAR[0], core) if p in NEAR else (p - CROSS[0], 1 - core)
            first, second = (near[side, holder, kv, v, :, cols(h)] for v in range(2))
            return jnp.where(which[p] == 1, second, first)
        return far[p - FAR[0], kv, :, cols(h)]

    def of_variant(p, ref, h):
        return ref[p if p in OWN else which[p], :, cols(h)]

    def pick(p, stats):
        return stats[p] if p in OWN else jnp.where(which[p] == 1, stats[1], stats[0])

    def merge(p, stats, new, combine, neutral):
        if p in OWN:
            stats[p] = combine(stats[p], new)
        else:
            for v in range(variants):
                stats[v] = combine(stats[v], jnp.where(which[p] == v, new, neutral))

    def per_head(shape, fill):
        return [[jnp.full(shape, fill, F32) for _ in range(variants)] for _ in range(heads)]

    tops = per_head((1, rows), NEGATIVE)

    def score(p):
        for h in range(heads):
            s = dot_nt(pair_kv(p, 0, h), of_variant(p, q_ref, h)) * scale
            if p not in OWN:
                s = jnp.where(live[p], s, NEGATIVE)
            scores[p, h] = s
            merge(p, tops[h], jnp.max(s, axis=0, keepdims=True), jnp.maximum, NEGATIVE)

    def grad_add(distance, first=False):
        sources = [t] if distance == 0 else [wrap(t - distance, RING)]
        if 0 < distance < 4:
            sources.append(wrap(t + distance, RING))
        for source in sources:
            columns = pl.ds(pl.multiple_of(source * width, width), width)
            piece = dot_nt(full[source].reshape(variants * rows, width), w_ref[:, columns])
            grad_sum[...] = piece if first else grad_sum[...] + piece

    for copy in loads:
        copy.wait()
    for p in OWN:
        score(p)
    grad_add(0, first=True)
    hop_on(1, 0)
    pass_on(0)
    hop_on(1, 1)
    sib_copies[0].wait_recv()
    for p in (SIB, *NEAR):
        score(p)
    grad_add(1)
    hop_on(2, 0)
    pass_on(1)
    hop_on(2, 1)
    for side in range(2):
        share_copies[side, 0].wait_recv()
    for p in CROSS:
        score(p)
    grad_add(2)
    hop_on(3, 0)
    for j in range(3):
        far_copies[j, 0].wait_recv()
    for p in (*FAR, ODD):
        score(p)
    hop_on(3, 1)
    sums = per_head((1, rows), 0.0)
    for p in range(PAIRS):
        for h in range(heads):
            e = jnp.exp(scores[p, h] - pick(p, tops[h]))
            scores[p, h] = e
            merge(p, sums[h], jnp.sum(e, axis=0, keepdims=True), jnp.add, 0.0)
    grad_add(3)
    inverse = [[1.0 / s for s in sums[h]] for h in range(heads)]
    sib_copies[1].wait_recv()
    for side in range(2):
        share_copies[side, 1].wait_recv()
    for j in range(3):
        far_copies[j, 1].wait_recv()
    for h in range(heads):
        outs = [jnp.zeros((rows, HD), F32) for _ in range(variants)]
        for p in range(PAIRS):
            prob = scores[p, h] * pick(p, inverse[h])
            scores[p, h] = prob
            merge(p, outs, dot_tn(prob.astype(BF16), pair_kv(p, 1, h)), jnp.add, 0.0)
        for v in range(variants):
            attended[v, :, cols(h)] = outs[v].astype(BF16)

    hop_on(4, 0, 1)
    share = width // RING
    half_rows = paired.shape[2]
    swaps = {}
    for j, r in enumerate(CORE_ORDER):
        chunk = wrap(y + r, RING)
        flat = attended[...].reshape(variants * rows, width)
        low = dot_tn(full[chunk].reshape(variants * rows, width), flat).astype(BF16)
        for b in range(RING):
            proj[b % 2, chunk, pl.ds((b // 2) * share, share)] = low[b * share:(b + 1) * share]
        swaps[r] = remote(
            proj.at[1 - core, chunk], pair_land.at[chunk], pair_send.at[j], pair_recv.at[j], (sib, t)
        )
    proj_begin, proj_advance, proj_result, proj_finish = ring_reduce(
        paired, proj_land, proj_send, proj_recv, y, lambda yy: at(yy, x, core)
    )

    layer_begin, layer_advance, layer_result, layer_finish = ring_reduce(
        part, layer_land, layer_send, layer_recv, t, lambda z: (d, z)
    )

    def pair_up(*chunks):
        for r in chunks:
            chunk = wrap(y + r, RING)
            swaps[r].wait_recv()
            for half in range(2):
                span = pl.ds(half * half_rows, half_rows)
                both = proj[core, chunk, span].astype(F32) + pair_land[chunk, span].astype(F32)
                paired[chunk, half] = both.astype(BF16)

    def layer_step(distance):
        for half in range(2):
            for side in range(2):
                layer_advance(distance, side, half)

    def proj_step(distance):
        for half in range(2):
            for side in range(2):
                proj_advance(distance, side, half)

    grad_add(4)
    grad[...] = grad_sum[...].astype(BF16).reshape(variants, rows, width)

    back = {}

    def send_back(p, kv):
        if p == SIB:
            slot, target, device = 0, sib_term.at[kv], sib
        elif p in CROSS:
            side = p - CROSS[0]
            slot, target, device = 1 + side, from_sib.at[side, kv], sib
        elif p in FAR:
            side = p - FAR[0]
            slot, target, device = 3 + side, from_far.at[side, kv], beside[side]
        elif p == ODD:
            slot, target, device = 5, from_far.at[2, kv], odd
        else:
            return
        back[slot, kv] = remote(
            term.at[p - SIB, kv], target, back_send.at[slot, kv], back_recv.at[slot, kv], (device, t)
        )

    deltas = per_head((1, rows), 0.0)

    def value_terms(*which_pairs):
        for p in which_pairs:
            for h in range(heads):
                prob = scores[p, h]
                low = prob.astype(BF16)
                gradient = of_variant(p, grad, h)
                dp = dot_nt(pair_kv(p, 1, h), gradient)
                prob_grads[p, h] = dp
                merge(p, deltas[h], jnp.sum(prob * dp, axis=0, keepdims=True), jnp.add, 0.0)
                value = dot_nn(low, gradient)
                if p in OWN:
                    own_term[1, p, :, cols(h)] = value
                else:
                    term[p - SIB, 1, :, cols(h)] = value.astype(BF16)
            send_back(p, 1)

    dqs = per_head((rows, HD), 0.0)

    def key_terms(*which_pairs):
        for p in which_pairs:
            for h in range(heads):
                ds = (scores[p, h] * (prob_grads[p, h] - pick(p, deltas[h])) * scale).astype(BF16)
                merge(p, dqs[h], dot_tn(ds, pair_kv(p, 0, h)), jnp.add, 0.0)
                value = dot_nn(ds, of_variant(p, q_ref, h))
                if p in OWN:
                    own_term[0, p, :, cols(h)] = value
                else:
                    term[p - SIB, 0, :, cols(h)] = value.astype(BF16)
            send_back(p, 0)

    home = {}
    sib_pick = [listed_in(lists_ref, counts_ref, 1, sib, b) == 1 for b in beside]
    own_pick = listed_in(lists_ref, counts_ref, 1, sib, d) == 1

    def relay_back(kv):
        for slot in range(1, 6):
            back[slot, kv].wait_recv()
        for side in range(2):
            parts = [
                (which[NEAR[side]] == 1, term[NEAR[side] - SIB, kv]),
                (sib_pick[side], from_sib[side, kv]),
                (relay_pick[side], from_far[side, kv]),
            ]
            extra = from_far[2, kv].astype(F32)
            extra = jnp.where(odd_side == side, extra, 0.0)
            both = [jnp.where(relay_pick[2], 0.0, extra), jnp.where(relay_pick[2], extra, 0.0)]
            for second, value in parts:
                value = value.astype(F32)
                both[0] = both[0] + jnp.where(second, 0.0, value)
                both[1] = both[1] + jnp.where(second, value, 0.0)
            for v in range(variants):
                relay_term[side, kv, v] = both[v].astype(BF16)
            home[side, kv] = remote(
                relay_term.at[side, kv], home_term.at[1 - side, kv],
                home_send.at[side, kv], home_recv.at[1 - side, kv], (beside[side], t),
            )

    value_terms(*FAR, ODD)
    for r in CORE_ORDER:
        target = wrap(t + r, RING)
        columns = pl.ds(pl.multiple_of(target * width, width), width)
        flat = attended[...].reshape(variants * rows, width)
        part[target] = dot_nn(flat, w_ref[:, columns]).astype(BF16).reshape(variants, rows, width)
        if r in (4, -3):
            layer_begin(abs(r))
    pair_up(4)
    proj_begin(4)
    pair_up(3, -3)
    proj_begin(3)
    value_terms(*CROSS, SIB, *NEAR, *OWN)
    key_terms(*FAR, ODD, *CROSS, SIB, *NEAR, *OWN)
    pair_up(2, -2)
    proj_step(4)
    pair_up(1, -1, 0)
    layer_step(4)
    proj_step(3)
    relay_back(1)
    layer_step(3)
    proj_step(2)
    relay_back(0)
    layer_step(2)
    proj_step(1)
    for h in range(heads):
        for v in range(variants):
            dq_ref[v, :, cols(h)] = dqs[h][v].astype(BF16)

    for half in range(2):
        piece = proj_result(half).astype(BF16)
        for i in range(half_rows // share):
            row_out[half * (half_rows // share) + i] = piece[i * share:(i + 1) * share]
    row_copies = []
    for s in range(1, ROW):
        xx = lax.rem(x + s, ROW)
        row_copies.append(remote(
            row_out.at[xx], row_land.at[s - 1], row_send.at[s - 1], row_recv.at[s - 1], at(y, xx, core)
        ))
    layer_step(1)
    for half in range(2):
        layer_ref[half] = layer_result(half).astype(BF16)
    for kv, out in ((1, dv_ref), (0, dk_ref)):
        back[0, kv].wait_recv()
        for side in range(2):
            home[1 - side, kv].wait_recv()
        value = sib_term[kv].astype(F32)
        for v in range(variants):
            mine = jnp.where(own_pick, value if v == 1 else 0.0, 0.0 if v == 1 else value)
            total = own_term[kv, v] + mine
            for side in range(2):
                total = total + home_term[side, kv, v].astype(F32)
            out[v] = total.astype(BF16)
    total = row_out[x].astype(F32)
    for s in range(ROW - 1):
        row_copies[s].wait_recv()
        total = total + row_land[s].astype(F32)
    proj_out[...] = total

    for group in (hops, near_copies, sib_copies, share_copies, far_copies, back, home):
        for copy in group.values():
            copy.wait_send()
    for copy in [*swaps.values(), *row_copies]:
        copy.wait_send()
    layer_finish()
    proj_finish()


def settle_kernel(*refs):
    count = len(refs) // 2
    for source, target in zip(refs[:count], refs[count:]):
        target[...] = source[...]


def local(queries, key_rows, value_rows, out_weight, out_grad, ibd_lists, ibd_counts):
    variants, rows, width = queries.shape
    heads = width // HD
    share = width // RING
    half_rows = ROW * share // 2
    smem = pl.BlockSpec(memory_space=pltpu.SMEM)
    vmem = pl.BlockSpec(memory_space=VMEM)
    anywhere = pl.BlockSpec(memory_space=pl.ANY)
    dma = pltpu.SemaphoreType.DMA
    block = (rows, width)
    outs = (
        jax.ShapeDtypeStruct((variants, *block), BF16),
        jax.ShapeDtypeStruct((variants, *block), BF16),
        jax.ShapeDtypeStruct((variants, *block), BF16),
        jax.ShapeDtypeStruct((variants, *block), BF16),
        jax.ShapeDtypeStruct((share, width), F32),
    )
    results = pl.pallas_call(
        whole_kernel,
        out_shape=outs,
        in_specs=[smem, smem] + [anywhere] * 5,
        out_specs=(vmem,) * 5,
        scratch_shapes=[
            VMEM((variants, *block), BF16),
            VMEM((2, variants, *block), BF16),
            VMEM(out_weight.shape, BF16),
            VMEM((RING, variants, *block), BF16),
            VMEM((2, variants, *block), BF16),
            VMEM((2, 2, 2, variants, *block), BF16),
            VMEM((3, 2, *block), BF16),
            VMEM((3, 2, *block), BF16),
            VMEM((variants * rows, width), F32),
            VMEM((variants, *block), BF16),
            VMEM((PAIRS, heads, rows, rows), F32),
            VMEM((PAIRS, heads, rows, rows), F32),
            VMEM((variants, *block), BF16),
            VMEM((RING, variants, *block), BF16),
            VMEM((2, RING, ROW * share, width), BF16),
            VMEM((2, 2, 4, *block), BF16),
            VMEM((RING, 2, half_rows, width), BF16),
            VMEM((RING, ROW * share, width), BF16),
            VMEM((2, 2, 4, half_rows, width), BF16),
            VMEM((ROW, share, width), BF16),
            VMEM((ROW - 1, share, width), BF16),
            VMEM((2, variants, *block), F32),
            VMEM((PAIRS - 2, 2, *block), BF16),
            VMEM((2, *block), BF16),
            VMEM((2, 2, *block), BF16),
            VMEM((3, 2, *block), BF16),
            VMEM((2, 2, variants, *block), BF16),
            VMEM((2, 2, variants, *block), BF16),
            dma((5,)),
            dma((2, 4, 2)), dma((2, 4, 2)),
            dma((2, 2)), dma((2, 2)), dma((2,)), dma((2,)), dma((2, 2)), dma((2, 2)),
            dma((3, 2)), dma((3, 2)), dma((6, 2)), dma((6, 2)), dma((2, 2)), dma((2, 2)),
            dma((2, 2, 4)), dma((2, 2, 4)), dma((8,)), dma((8,)),
            dma((2, 2, 4)), dma((2, 2, 4)), dma((ROW - 1,)), dma((ROW - 1,)),
        ],
        compiler_params=pltpu.CompilerParams(
            collective_id=0, has_side_effects=True, vmem_limit_bytes=60 * 1024 * 1024
        ),
        name="whole",
    )(
        jnp.transpose(ibd_lists, (2, 0, 1)), ibd_counts,
        queries, key_rows, value_rows, out_weight, out_grad,
    )
    return pl.pallas_call(
        settle_kernel,
        out_shape=outs,
        in_specs=[vmem] * 5,
        out_specs=(vmem,) * 5,
        name="settle",
    )(*results)


def solution(mesh):
    spec = P(None, "dp", "tensor")
    return jax.shard_map(
        local,
        mesh=mesh,
        in_specs=(spec, spec, spec, P("tensor", None), spec, P(), P()),
        out_specs=(spec, spec, spec, spec, P("dp", "tensor")),
        check_vma=False,
    )
```
